1024 devices in a mesh: gx: 16 (over z_lo, core), gy: 16 (over y, z_hi), gz: 4 (over x).
Axes of the slice: x: 4, y: 4, z: 32 (z_hi: 4, z_lo: 8; z = z_hi * 8 + z_lo), core: 2. Of those that a mesh axis runs over, the one named last changes fastest.
Arguments:
- fine_multipoles: bfloat16 [64, 64, 32, 64], P('gx', 'gy', 'gz'), may hold values from -6 to 6
- fine_translations: bfloat16 [158, 64, 64], replicated, may hold values from -0.0546875 to 0.0546875
- coarse_multipoles: bfloat16 [64, 64, 16, 64], P('gx', 'gy', 'gz'), may hold values from -6 to 6
- coarse_translations: bfloat16 [158, 64, 64], replicated, may hold values from -0.0546875 to 0.0546875
Outputs:
- fine_locals: float32 [64, 64, 32, 64], P('gx', 'gy', 'gz')
- coarse_locals: float32 [64, 64, 16, 64], P('gx', 'gy', 'gz')
The draws below stay inside these ranges and needn't reach their ends.
All inputs are finite; a program needn't handle non-finite values.
Results may differ from the reference program's by a relative error of at most 0.00045.
Values may be sent and summed in bfloat16 or wider, within the bound.
A program may use at most 128 MiB of HBM per device.

```python
import jax
import jax.numpy as jnp
import numpy as np
from jax import lax

COEFFS = 64
OFFSETS = 158
FINE_NX = 64
FINE_NY = 64
FINE_NZ = 32
COARSE_NX = 64
COARSE_NY = 64
COARSE_NZ = 16


def level_of(key, dims, shards, smallest, top_value):
    level, own = 1.0, jax.random.fold_in(key, 6)
    for dim, blocks in shards:
        draws = jnp.exp(jax.random.uniform(jax.random.fold_in(own, dim), (blocks,), jnp.float32, smallest / len(shards), top_value / len(shards)))
        level = level * jnp.repeat(draws, dims[dim] // blocks).reshape([-1 if axis == dim else 1 for axis in range(len(dims))])
    return level


def bell_draw(rng, shape, scale, reach, split=(), kind=jnp.bfloat16):
    gain = level_of(rng, shape, split, -0.22, 0.18) if split else 1.0
    drawn = jax.random.normal(rng, shape, jnp.float32) * scale * gain
    return jnp.minimum(jnp.maximum(drawn, -reach), reach).astype(kind)


def setup_inputs(seed: int = 0) -> dict:
    seeds = jax.random.split(jax.random.key(seed), 5)
    fine_multipoles = bell_draw(seeds[0], (FINE_NX, FINE_NY, FINE_NZ, COEFFS), 1.0, 6.0, ((0, 16), (1, 16), (2, 4)))
    fine_translations = bell_draw(seeds[1], (OFFSETS, COEFFS, COEFFS), (COEFFS * 189) ** -0.5, 0.0546875)
    coarse_multipoles = bell_draw(seeds[2], (COARSE_NX, COARSE_NY, COARSE_NZ, COEFFS), 1.0, 6.0, ((0, 16), (1, 16), (2, 4)))
    coarse_translations = bell_draw(seeds[3], (OFFSETS, COEFFS, COEFFS), (COEFFS * 189) ** -0.5, 0.0546875)
    return dict(fine_multipoles=fine_multipoles, fine_translations=fine_translations, coarse_multipoles=coarse_multipoles, coarse_translations=coarse_translations)


def half_offsets():
    listed = []
    for step_x in range(-3, 4):
        for step_y in range(-3, 4):
            for step_z in range(-3, 4):
                if max(abs(step_x), abs(step_y), abs(step_z)) < 2:
                    continue
                if step_x > 0 or (step_x == 0 and (step_y > 0 or (step_y == 0 and step_z > 0))):
                    listed.append((step_x, step_y, step_z))
    return listed


def allowed(coords, offset):
    return (jnp.abs(jnp.floor_divide(coords + offset, 2) - jnp.floor_divide(coords, 2)) <= 1).astype(jnp.float32)


def level_locals(multipoles, translations):
    span_x, span_y, span_z, coeffs = multipoles.shape
    widened = jnp.pad(multipoles.astype(jnp.float32), ((3, 3), (3, 3), (3, 3), (0, 0)))
    table = jnp.asarray(np.array(half_offsets(), dtype=np.int32))
    first = jnp.arange(span_x, dtype=jnp.int32)
    second = jnp.arange(span_y, dtype=jnp.int32)
    third = jnp.arange(span_z, dtype=jnp.int32)

    def advance(total, item):
        offset, matrix = item
        matrix = matrix.astype(jnp.float32)
        zero = jnp.zeros((), jnp.int32)
        ahead = lax.dynamic_slice(widened, (3 + offset[0], 3 + offset[1], 3 + offset[2], zero), (span_x, span_y, span_z, coeffs))
        behind = lax.dynamic_slice(widened, (3 - offset[0], 3 - offset[1], 3 - offset[2], zero), (span_x, span_y, span_z, coeffs))
        keep = allowed(first, offset[0])[:, None, None] * allowed(second, offset[1])[None, :, None] * allowed(third, offset[2])[None, None, :]
        keep_back = allowed(first - offset[0], offset[0])[:, None, None] * allowed(second - offset[1], offset[1])[None, :, None] * allowed(third - offset[2], offset[2])[None, None, :]
        term_ahead = jnp.dot(ahead.reshape(-1, coeffs), matrix.T, precision=lax.Precision.HIGHEST).reshape(span_x, span_y, span_z, coeffs)
        term_behind = jnp.dot(behind.reshape(-1, coeffs), matrix, precision=lax.Precision.HIGHEST).reshape(span_x, span_y, span_z, coeffs)
        return total + keep[..., None] * term_ahead + keep_back[..., None] * term_behind, None

    start = jnp.zeros((span_x, span_y, span_z, coeffs), jnp.float32)
    total, unused = lax.scan(advance, start, (table, translations))
    return total


def reference(fine_multipoles, fine_translations, coarse_multipoles, coarse_translations):
    fine_locals = level_locals(fine_multipoles, fine_translations)
    coarse_locals = level_locals(coarse_multipoles, coarse_translations)
    return (fine_locals, coarse_locals)
```

```python
import functools

import jax
import jax.numpy as jnp
import numpy as np
from jax import lax
from jax.experimental import pallas as pl
from jax.experimental.pallas import tpu as pltpu
from jax.sharding import PartitionSpec as P

MESH = pl.DeviceIdType.MESH
BF16 = jnp.bfloat16
F32 = jnp.float32

GROUPS = [(0, ey) for ey in range(4)] + [(ex, ey) for ex in range(1, 4) for ey in range(-3, 4)]
PLACES = 7 * len(GROUPS)
Y_PAIRS = ((-3, -2), (-1, 0), (1, 2), (3,))
PLANE = [(sx, sz) for sx in (-1, 0, 1) for sz in (-1, 0, 1) if (sx, sz) != (0, 0)]
FINE_SLOTS = (0, 2, 4, 5, 6, 8)
COARSE_SLOTS = (1, 3, 7, 9)
SLOTS = 10


def group(ex, ey):
    return ey if ex == 0 else 4 + (ex - 1) * 7 + ey + 3


def half_offsets():
    listed = []
    for step_x in range(-3, 4):
        for step_y in range(-3, 4):
            for step_z in range(-3, 4):
                if max(abs(step_x), abs(step_y), abs(step_z)) < 2:
                    continue
                if step_x > 0 or (step_x == 0 and (step_y > 0 or (step_y == 0 and step_z > 0))):
                    listed.append((step_x, step_y, step_z))
    return listed


def table_runs():
    places = [group(x, y) * 7 + z + 3 for x, y, z in half_offsets()]
    runs = []
    for index, place in enumerate(places):
        cut = place in (4 * 7, 11 * 7, 18 * 7)
        if runs and runs[-1][1] + runs[-1][2] == place and not cut:
            runs[-1][2] += 1
        else:
            runs.append([index, place, 1])
    empty = [place for place in range(PLACES) if place not in set(places)]
    return [tuple(run) for run in runs], empty


RUNS, EMPTY = table_runs()


def pack_level(src, stage, own, up, down, nz, base, msg_base):
    zp = nz // 2
    stage[0 : 16 * nz, 0:64] = src[...].astype(F32).reshape(16 * nz, 64)
    for x in range(4):
        for y in range(4):
            row = (x * 4 + y) * nz
            even = stage[pl.ds(row, zp, stride=2), 0:64]
            odd = stage[pl.ds(row + 1, zp, stride=2), 0:64]
            both = jnp.concatenate([even, odd], axis=1)
            tile = (x // 2) * zp * 2 + x % 2
            own[pl.ds(base + tile * 8 + 2 + y, zp, stride=16), :] = both
            face = up if y >= 2 else down
            face[pl.ds(msg_base + tile * 2 + y % 2, zp, stride=4), :] = both


def unpack_level(dst, tiles, nz):
    zp = nz // 2
    for x in range(4):
        for y in range(4):
            start = ((x // 2) * zp * 2 + x % 2) * 8 + y
            both = tiles[pl.ds(start, zp, stride=16), :]
            dst[x, y, pl.ds(0, zp, stride=2), :] = both[:, 0:64]
            dst[x, y, pl.ds(1, zp, stride=2), :] = both[:, 64:128]


def build_weights(places, ahead, behind, first, last):
    @pl.loop(first, last)
    def _(g):
        blocks = [places[g * 7 + e] for e in range(7)]
        for j in range(6):
            pair = jnp.concatenate([blocks[j], blocks[j + 1]], axis=1)
            half = 64 if j % 2 == 0 else 0
            ahead[g, half : half + 64, (j // 2) * 128 : (j // 2) * 128 + 128] = pair
            behind[g, (5 - j) * 64 : (5 - j) * 64 + 64, :] = pair


def shift_tiles(halo, odd, high, low):
    zero = jnp.zeros((8, 128), F32)

    @pl.loop(0, SLOTS)
    def _(s):
        wide = [halo[q, s].astype(F32) for q in range(4)]
        for q in range(3):
            odd[q, s] = jnp.concatenate([wide[q][8:16], wide[q + 1][0:8]], axis=0).astype(BF16)
        for q in range(2):
            high[q, s] = jnp.concatenate([wide[q + 2][8:16], zero], axis=0).astype(BF16)
            low[q, s] = jnp.concatenate([zero, wide[q][0:8]], axis=0).astype(BF16)


def sources(halo, odd, high, low, dx, slots):
    if dx % 2 == 0:
        part, first = halo, 1 + dx // 2
    elif dx == 3:
        part, first = high, 0
    elif dx == -3:
        part, first = low, 0
    else:
        part, first = odd, (dx + 1) // 2
    zp = len(slots) - 2
    columns = []
    for step in range(3):
        columns.append(
            jnp.concatenate([part[first + q, slots[z + step]] for q in range(2) for z in range(zp)], axis=0)
        )
    return jnp.concatenate(columns, axis=1)


def dot_ahead(left, weights):
    return lax.dot_general(left, weights, (((1,), (1,)), ((), ())), preferred_element_type=F32)


def dot_behind(left, weights):
    return lax.dot_general(left, weights, (((1,), (0,)), ((), ())), preferred_element_type=F32)


def level(halo, odd, high, low, ahead, behind, slots):
    get = functools.partial(sources, halo, odd, high, low, slots=slots)
    forward = {x: get(x) for x in range(0, 4)}
    backward = {x: get(-x) for x in range(0, 4)}
    rows = forward[0].shape[0]
    y = lax.broadcasted_iota(jnp.int32, (rows // 8, 8, 128), 1)
    total = None
    for pair in Y_PAIRS:
        xs = range(0, 4) if min(pair) >= 0 else range(1, 4)
        left = jnp.concatenate([forward[x] for x in xs], axis=1)
        right = jnp.concatenate(
            [jnp.concatenate([ahead[group(x, ey)] for x in xs], axis=1) for ey in pair], axis=0
        )
        sums = dot_ahead(left, right)
        xs = range(0, 4) if max(pair) <= 0 else range(1, 4)
        left = jnp.concatenate([backward[x] for x in xs], axis=1)
        right = jnp.concatenate(
            [jnp.concatenate([behind[group(x, -ey)] for x in xs], axis=0) for ey in pair], axis=1
        )
        sums = sums + dot_behind(left, right)
        for place, ey in enumerate(pair):
            term = sums[:, place * 128 : place * 128 + 128]
            if ey == 0:
                term = term + dot_ahead(forward[0], ahead[group(0, 0)])
            term = term.reshape(rows // 8, 8, 128)
            term = pltpu.roll(term, (-(2 + ey)) % 8, 1)
            if ey == 3:
                term = jnp.where(y % 2 == 0, term, 0.0)
            if ey == -3:
                term = jnp.where(y % 2 == 1, term, 0.0)
            total = term if total is None else total + term
    return total.reshape(rows, 128)


def kernel(
    sizes, fine, fine_table, coarse, coarse_table, fine_out, coarse_out,
    fine_places, coarse_places, fine_ahead, fine_behind, coarse_ahead, coarse_behind,
    halo, odd, high, low, stage, own, faces, sent, got, spread, tiles,
    table_sem, y_send, y_recv, plane_send, plane_recv,
):
    nx, ny, nz = sizes
    gx, gy, gz = lax.axis_index("gx"), lax.axis_index("gy"), lax.axis_index("gz")

    copies = []
    for at, (table, places) in enumerate(((fine_table, fine_places), (coarse_table, coarse_places))):
        copies.append([
            pltpu.make_async_copy(
                table.at[pl.ds(c, n)], places.at[pl.ds(p, n)], table_sem.at[at, k]
            )
            for k, (c, p, n) in enumerate(RUNS)
        ])
    for some in copies:
        for copy in some:
            copy.start()

    @pl.when(gx == 0)
    def _():
        halo[0] = jnp.zeros((SLOTS, 16, 128), BF16)

    @pl.when(gx == nx - 1)
    def _():
        halo[3] = jnp.zeros((SLOTS, 16, 128), BF16)

    @pl.when(gz == 0)
    def _():
        halo[:, 0:2] = jnp.zeros((4, 2, 16, 128), BF16)

    @pl.when(gz == nz - 1)
    def _():
        halo[:, 8:10] = jnp.zeros((4, 2, 16, 128), BF16)

    @pl.when(gy == 0)
    def _():
        got[0] = jnp.zeros((48, 128), BF16)

    @pl.when(gy == ny - 1)
    def _():
        got[1] = jnp.zeros((48, 128), BF16)

    def in_y(sy):
        return (gy + sy >= 0) & (gy + sy < ny)

    def in_plane(sx, sz):
        return (gx + sx >= 0) & (gx + sx < nx) & (gz + sz >= 0) & (gz + sz < nz)

    def at_y(sy):
        return (gx, lax.rem(gy + sy + ny, ny), gz)

    def at_plane(sx, sz):
        return (lax.rem(gx + sx + nx, nx), gy, lax.rem(gz + sz + nz, nz))

    barrier = pltpu.get_barrier_semaphore()
    neighbours = jnp.int32(0)
    for sy in (1, -1):
        neighbours += in_y(sy).astype(jnp.int32)

        @pl.when(in_y(sy))
        def _():
            pl.semaphore_signal(barrier, inc=1, device_id=at_y(sy), device_id_type=MESH)

    for sx, sz in PLANE:
        neighbours += in_plane(sx, sz).astype(jnp.int32)

        @pl.when(in_plane(sx, sz))
        def _():
            pl.semaphore_signal(barrier, inc=1, device_id=at_plane(sx, sz), device_id_type=MESH)

    pack_level(fine, stage, own, faces.at[0], faces.at[1], 8, 0, 0)
    pack_level(coarse, stage, own, faces.at[0], faces.at[1], 4, 128, 32)
    sent[...] = faces[...].astype(BF16)

    y_copies = [
        (sy, -sy, pltpu.make_async_remote_copy(
            src_ref=sent.at[k], dst_ref=got.at[k], send_sem=y_send.at[k], recv_sem=y_recv.at[k],
            device_id=at_y(sy), device_id_type=MESH,
        ))
        for k, sy in enumerate((1, -1))
    ]
    pl.semaphore_wait(barrier, neighbours)
    for to, _, copy in y_copies:

        @pl.when(in_y(to))
        def _():
            copy.start()

    for places in (fine_places, coarse_places):
        for place in EMPTY:
            places[place] = jnp.zeros((64, 64), BF16)
    for copy in copies[0]:
        copy.wait()
    build_weights(fine_places, fine_ahead, fine_behind, 0, len(GROUPS))

    for _, back, copy in y_copies:

        @pl.when(in_y(back))
        def _():
            copy.wait_recv()

    spread[...] = got[...].astype(F32)
    for row in range(2):
        own[pl.ds(row, 24, stride=8), :] = spread[0, pl.ds(row, 24, stride=2), :]
        own[pl.ds(6 + row, 24, stride=8), :] = spread[1, pl.ds(row, 24, stride=2), :]
    for q in range(2):
        for slots, zp, base in ((FINE_SLOTS, 4, 0), (COARSE_SLOTS, 2, 128)):
            for z in range(zp):
                start = base + (q * zp + z) * 16
                halo[1 + q, slots[1 + z]] = own[start : start + 16, :].astype(BF16)

    plane_copies = []
    for k, (sx, sz) in enumerate(PLANE):
        x_from, x_to, x_count = {-1: (1, 3, 1), 0: (1, 1, 2), 1: (2, 0, 1)}[sx]
        z_from, z_to, z_count = {-1: (2, 8, 2), 0: (2, 2, 6), 1: (6, 0, 2)}[sz]
        plane_copies.append((
            sx, sz, pltpu.make_async_remote_copy(
                src_ref=halo.at[pl.ds(x_from, x_count), pl.ds(z_from, z_count)],
                dst_ref=halo.at[pl.ds(x_to, x_count), pl.ds(z_to, z_count)],
                send_sem=plane_send.at[k], recv_sem=plane_recv.at[k],
                device_id=at_plane(sx, sz), device_id_type=MESH,
            )
        ))
    for sx, sz, copy in plane_copies:

        @pl.when(in_plane(sx, sz))
        def _():
            copy.start()

    for copy in copies[1]:
        copy.wait()
    build_weights(coarse_places, coarse_ahead, coarse_behind, 0, len(GROUPS))

    for sx, sz, copy in plane_copies:

        @pl.when(in_plane(-sx, -sz))
        def _():
            copy.wait_recv()

    shift_tiles(halo, odd, high, low)
    tiles[...] = level(halo, odd, high, low, fine_ahead, fine_behind, FINE_SLOTS)
    unpack_level(fine_out, tiles, 8)
    tiles[0:64, :] = level(halo, odd, high, low, coarse_ahead, coarse_behind, COARSE_SLOTS)
    unpack_level(coarse_out, tiles, 4)

    for to, _, copy in y_copies:

        @pl.when(in_y(to))
        def _():
            copy.wait_send()

    for sx, sz, copy in plane_copies:

        @pl.when(in_plane(sx, sz))
        def _():
            copy.wait_send()


def body(sizes, fine_multipoles, fine_translations, coarse_multipoles, coarse_translations):
    vmem = pl.BlockSpec(memory_space=pltpu.VMEM)
    hbm = pl.BlockSpec(memory_space=pl.ANY)
    groups = len(GROUPS)
    return pl.pallas_call(
        functools.partial(kernel, sizes),
        out_shape=[
            jax.ShapeDtypeStruct(fine_multipoles.shape, F32),
            jax.ShapeDtypeStruct(coarse_multipoles.shape, F32),
        ],
        in_specs=[vmem, hbm, vmem, hbm],
        out_specs=[vmem, vmem],
        scratch_shapes=[
            pltpu.VMEM((PLACES, 64, 64), BF16),
            pltpu.VMEM((PLACES, 64, 64), BF16),
            pltpu.VMEM((groups, 128, 384), BF16),
            pltpu.VMEM((groups, 384, 128), BF16),
            pltpu.VMEM((groups, 128, 384), BF16),
            pltpu.VMEM((groups, 384, 128), BF16),
            pltpu.VMEM((4, SLOTS, 16, 128), BF16),
            pltpu.VMEM((3, SLOTS, 16, 128), BF16),
            pltpu.VMEM((2, SLOTS, 16, 128), BF16),
            pltpu.VMEM((2, SLOTS, 16, 128), BF16),
            pltpu.VMEM((128, 128), F32),
            pltpu.VMEM((192, 128), F32),
            pltpu.VMEM((2, 48, 128), F32),
            pltpu.VMEM((2, 48, 128), BF16),
            pltpu.VMEM((2, 48, 128), BF16),
            pltpu.VMEM((2, 48, 128), F32),
            pltpu.VMEM((128, 128), F32),
            pltpu.SemaphoreType.DMA((2, len(RUNS))),
            pltpu.SemaphoreType.DMA((2,)),
            pltpu.SemaphoreType.DMA((2,)),
            pltpu.SemaphoreType.DMA((8,)),
            pltpu.SemaphoreType.DMA((8,)),
        ],
        compiler_params=pltpu.CompilerParams(
            collective_id=0, has_side_effects=True, vmem_limit_bytes=40 * 1024 * 1024
        ),
        name="translate",
    )(fine_multipoles, fine_translations, coarse_multipoles, coarse_translations)


def solution(mesh):
    sizes = tuple(mesh.shape[axis] for axis in ("gx", "gy", "gz"))
    return jax.shard_map(
        functools.partial(body, sizes),
        mesh=mesh,
        in_specs=(P("gx", "gy", "gz", None), P(), P("gx", "gy", "gz", None), P()),
        out_specs=(P("gx", "gy", "gz", None), P("gx", "gy", "gz", None)),
        check_vma=False,
    )
```

```python
import functools

import jax
import jax.numpy as jnp
import numpy as np
from jax import lax
from jax.experimental import pallas as pl
from jax.experimental.pallas import tpu as pltpu
from jax.sharding import PartitionSpec as P

MESH = pl.DeviceIdType.MESH
BF16 = jnp.bfloat16
F32 = jnp.float32

GROUPS = [(0, ey) for ey in range(4)] + [(ex, ey) for ex in range(1, 4) for ey in range(-3, 4)]
OFFSETS = 158
Y_PAIRS = ((-3, -2), (-1, 0), (1, 2), (3,))
PLANE = [(sx, sz) for sx in (-1, 0, 1) for sz in (-1, 0, 1) if (sx, sz) != (0, 0)]
FINE_SLOTS = (0, 2, 4, 5, 6, 8)
COARSE_SLOTS = (1, 3, 7, 9)
SLOTS = 10


def group(ex, ey):
    return ey if ex == 0 else 4 + (ex - 1) * 7 + ey + 3


def half_offsets():
    listed = []
    for step_x in range(-3, 4):
        for step_y in range(-3, 4):
            for step_z in range(-3, 4):
                if max(abs(step_x), abs(step_y), abs(step_z)) < 2:
                    continue
                if step_x > 0 or (step_x == 0 and (step_y > 0 or (step_y == 0 and step_z > 0))):
                    listed.append((step_x, step_y, step_z))
    return listed


def place_selection():
    picks = np.zeros((8 * len(GROUPS), OFFSETS), np.float32)
    for index, (x, y, z) in enumerate(half_offsets()):
        picks[8 * group(x, y) + z + 3, index] = 1.0
    return picks


def pack_level(src, stage, own, up, down, nz, base, msg_base):
    zp = nz // 2
    stage[0 : 16 * nz, 0:64] = src[...].astype(F32).reshape(16 * nz, 64)
    for x in range(4):
        for y in range(4):
            row = (x * 4 + y) * nz
            even = stage[pl.ds(row, zp, stride=2), 0:64]
            odd = stage[pl.ds(row + 1, zp, stride=2), 0:64]
            both = jnp.concatenate([even, odd], axis=1)
            tile = (x // 2) * zp * 2 + x % 2
            own[pl.ds(base + tile * 8 + 2 + y, zp, stride=16), :] = both
            face = up if y >= 2 else down
            face[pl.ds(msg_base + tile * 2 + y % 2, zp, stride=4), :] = both


def unpack_level(dst, tiles, nz):
    zp = nz // 2
    for x in range(4):
        for y in range(4):
            start = ((x // 2) * zp * 2 + x % 2) * 8 + y
            both = tiles[pl.ds(start, zp, stride=16), :]
            dst[x, y, pl.ds(0, zp, stride=2), :] = both[:, 0:64]
            dst[x, y, pl.ds(1, zp, stride=2), :] = both[:, 64:128]


def turn_table(picks, table, turned, first, last):
    @pl.loop(first, last)
    def _(r):
        rows = jnp.concatenate([table[r], table[32 + r]], axis=0)
        classes = dot_ahead(picks[...], rows)
        for g in range(len(GROUPS)):
            turned[pl.ds(pl.multiple_of(g * 256 + r * 8, 8), 8), :] = classes[g * 8 : g * 8 + 8]


def build_weights(turned, weights, first, last):
    left = lax.broadcasted_iota(jnp.int32, (32, 128), 1) < 64

    @pl.loop(first, last)
    def _(g):
        blocks = [turned[pl.ds(g * 256 + e, 32, stride=8), :] for e in range(7)]
        swapped = [pltpu.roll(block, 64, 1) for block in blocks]
        for j in range(6):
            weights[g, j, 0:32] = jnp.where(left, blocks[j], swapped[j + 1]).astype(BF16)
            weights[g, j, 32:64] = jnp.where(left, swapped[j], blocks[j + 1]).astype(BF16)


def ahead(weights, g):
    rows = [jnp.concatenate([weights[g, j + 2 * step] for step in range(3)], axis=1) for j in (1, 0)]
    return jnp.concatenate(rows, axis=0)


def behind(weights, g):
    return jnp.concatenate([weights[g, 5 - s] for s in range(6)], axis=0)


def shift_tiles(halo, odd, high, low):
    zero = jnp.zeros((8, 128), F32)

    @pl.loop(0, SLOTS)
    def _(s):
        wide = [halo[q, s].astype(F32) for q in range(4)]
        for q in range(3):
            odd[q, s] = jnp.concatenate([wide[q][8:16], wide[q + 1][0:8]], axis=0).astype(BF16)
        for q in range(2):
            high[q, s] = jnp.concatenate([wide[q + 2][8:16], zero], axis=0).astype(BF16)
            low[q, s] = jnp.concatenate([zero, wide[q][0:8]], axis=0).astype(BF16)


def sources(halo, odd, high, low, dx, slots):
    if dx % 2 == 0:
        part, first = halo, 1 + dx // 2
    elif dx == 3:
        part, first = high, 0
    elif dx == -3:
        part, first = low, 0
    else:
        part, first = odd, (dx + 1) // 2
    zp = len(slots) - 2
    columns = []
    for step in range(3):
        columns.append(
            jnp.concatenate([part[first + q, slots[z + step]] for q in range(2) for z in range(zp)], axis=0)
        )
    return jnp.concatenate(columns, axis=1)


def dot_ahead(left, weights):
    return lax.dot_general(left, weights, (((1,), (1,)), ((), ())), preferred_element_type=F32)


def dot_behind(left, weights):
    return lax.dot_general(left, weights, (((1,), (0,)), ((), ())), preferred_element_type=F32)


def level(halo, odd, high, low, weights, slots):
    get = functools.partial(sources, halo, odd, high, low, slots=slots)
    forward = {x: get(x) for x in range(0, 4)}
    backward = {x: get(-x) for x in range(0, 4)}
    rows = forward[0].shape[0]
    y = lax.broadcasted_iota(jnp.int32, (rows // 8, 8, 128), 1)
    total = None
    for pair in Y_PAIRS:
        xs = range(0, 4) if min(pair) >= 0 else range(1, 4)
        left = jnp.concatenate([forward[x] for x in xs], axis=1)
        right = jnp.concatenate(
            [jnp.concatenate([ahead(weights, group(x, ey)) for x in xs], axis=1) for ey in pair], axis=0
        )
        sums = dot_ahead(left, right)
        xs = range(0, 4) if max(pair) <= 0 else range(1, 4)
        left = jnp.concatenate([backward[x] for x in xs], axis=1)
        right = jnp.concatenate(
            [jnp.concatenate([behind(weights, group(x, -ey)) for x in xs], axis=0) for ey in pair], axis=1
        )
        sums = sums + dot_behind(left, right)
        for place, ey in enumerate(pair):
            term = sums[:, place * 128 : place * 128 + 128]
            if ey == 0:
                term = term + dot_ahead(forward[0], ahead(weights, group(0, 0)))
            term = term.reshape(rows // 8, 8, 128)
            term = pltpu.roll(term, (-(2 + ey)) % 8, 1)
            if ey == 3:
                term = jnp.where(y % 2 == 0, term, 0.0)
            if ey == -3:
                term = jnp.where(y % 2 == 1, term, 0.0)
            total = term if total is None else total + term
    return total.reshape(rows, 128)


def kernel(
    sizes, picks, fine_hbm, fine_table_hbm, coarse_hbm, coarse_table_hbm, fine_out, coarse_out,
    fine, coarse, fine_table, coarse_table, turned, fine_weights, coarse_weights,
    halo, odd, high, low, stage, own, faces, sent, got, spread, tiles,
    load_sem, y_send, y_recv, plane_send, plane_recv,
):
    nx, ny, nz = sizes
    gx, gy, gz = lax.axis_index("gx"), lax.axis_index("gy"), lax.axis_index("gz")

    loads = [
        pltpu.make_async_copy(src, dst, load_sem.at[k])
        for k, (src, dst) in enumerate((
            (fine_hbm, fine), (coarse_hbm, coarse),
            (fine_table_hbm, fine_table), (coarse_table_hbm, coarse_table),
        ))
    ]
    for load in loads:
        load.start()

    @pl.when(gx == 0)
    def _():
        halo[0] = jnp.zeros((SLOTS, 16, 128), BF16)

    @pl.when(gx == nx - 1)
    def _():
        halo[3] = jnp.zeros((SLOTS, 16, 128), BF16)

    @pl.when(gz == 0)
    def _():
        halo[:, 0:2] = jnp.zeros((4, 2, 16, 128), BF16)

    @pl.when(gz == nz - 1)
    def _():
        halo[:, 8:10] = jnp.zeros((4, 2, 16, 128), BF16)

    @pl.when(gy == 0)
    def _():
        got[0] = jnp.zeros((48, 128), BF16)

    @pl.when(gy == ny - 1)
    def _():
        got[1] = jnp.zeros((48, 128), BF16)

    def in_y(sy):
        return (gy + sy >= 0) & (gy + sy < ny)

    def in_plane(sx, sz):
        return (gx + sx >= 0) & (gx + sx < nx) & (gz + sz >= 0) & (gz + sz < nz)

    def at_y(sy):
        return (gx, lax.rem(gy + sy + ny, ny), gz)

    def at_plane(sx, sz):
        return (lax.rem(gx + sx + nx, nx), gy, lax.rem(gz + sz + nz, nz))

    barrier = pltpu.get_barrier_semaphore()
    neighbours = jnp.int32(0)
    for sy in (1, -1):
        neighbours += in_y(sy).astype(jnp.int32)

        @pl.when(in_y(sy))
        def _():
            pl.semaphore_signal(barrier, inc=1, device_id=at_y(sy), device_id_type=MESH)

    for sx, sz in PLANE:
        neighbours += in_plane(sx, sz).astype(jnp.int32)

        @pl.when(in_plane(sx, sz))
        def _():
            pl.semaphore_signal(barrier, inc=1, device_id=at_plane(sx, sz), device_id_type=MESH)

    loads[0].wait()
    loads[1].wait()
    pack_level(fine, stage, own, faces.at[0], faces.at[1], 8, 0, 0)
    pack_level(coarse, stage, own, faces.at[0], faces.at[1], 4, 128, 32)
    sent[...] = faces[...].astype(BF16)

    y_copies = [
        (sy, -sy, pltpu.make_async_remote_copy(
            src_ref=sent.at[k], dst_ref=got.at[k], send_sem=y_send.at[k], recv_sem=y_recv.at[k],
            device_id=at_y(sy), device_id_type=MESH,
        ))
        for k, sy in enumerate((1, -1))
    ]
    pl.semaphore_wait(barrier, neighbours)
    for to, _, copy in y_copies:

        @pl.when(in_y(to))
        def _():
            copy.start()

    loads[2].wait()
    turn_table(picks, fine_table, turned, 0, 32)
    build_weights(turned, fine_weights, 0, len(GROUPS))

    for _, back, copy in y_copies:

        @pl.when(in_y(back))
        def _():
            copy.wait_recv()

    spread[...] = got[...].astype(F32)
    for row in range(2):
        own[pl.ds(row, 24, stride=8), :] = spread[0, pl.ds(row, 24, stride=2), :]
        own[pl.ds(6 + row, 24, stride=8), :] = spread[1, pl.ds(row, 24, stride=2), :]
    for q in range(2):
        for slots, zp, base in ((FINE_SLOTS, 4, 0), (COARSE_SLOTS, 2, 128)):
            for z in range(zp):
                start = base + (q * zp + z) * 16
                halo[1 + q, slots[1 + z]] = own[start : start + 16, :].astype(BF16)

    plane_copies = []
    for k, (sx, sz) in enumerate(PLANE):
        x_from, x_to, x_count = {-1: (1, 3, 1), 0: (1, 1, 2), 1: (2, 0, 1)}[sx]
        z_from, z_to, z_count = {-1: (2, 8, 2), 0: (2, 2, 6), 1: (6, 0, 2)}[sz]
        plane_copies.append((
            sx, sz, pltpu.make_async_remote_copy(
                src_ref=halo.at[pl.ds(x_from, x_count), pl.ds(z_from, z_count)],
                dst_ref=halo.at[pl.ds(x_to, x_count), pl.ds(z_to, z_count)],
                send_sem=plane_send.at[k], recv_sem=plane_recv.at[k],
                device_id=at_plane(sx, sz), device_id_type=MESH,
            )
        ))
    for sx, sz, copy in plane_copies:

        @pl.when(in_plane(sx, sz))
        def _():
            copy.start()

    loads[3].wait()
    turn_table(picks, coarse_table, turned, 0, 32)
    build_weights(turned, coarse_weights, 0, len(GROUPS))

    for sx, sz, copy in plane_copies:

        @pl.when(in_plane(-sx, -sz))
        def _():
            copy.wait_recv()

    shift_tiles(halo, odd, high, low)
    tiles[...] = level(halo, odd, high, low, fine_weights, FINE_SLOTS)
    unpack_level(fine_out, tiles, 8)
    tiles[0:64, :] = level(halo, odd, high, low, coarse_weights, COARSE_SLOTS)
    unpack_level(coarse_out, tiles, 4)

    for to, _, copy in y_copies:

        @pl.when(in_y(to))
        def _():
            copy.wait_send()

    for sx, sz, copy in plane_copies:

        @pl.when(in_plane(sx, sz))
        def _():
            copy.wait_send()


def body(sizes, fine_multipoles, fine_translations, coarse_multipoles, coarse_translations):
    vmem = pl.BlockSpec(memory_space=pltpu.VMEM)
    hbm = pl.BlockSpec(memory_space=pl.ANY)
    groups = len(GROUPS)
    return pl.pallas_call(
        functools.partial(kernel, sizes),
        out_shape=[
            jax.ShapeDtypeStruct(fine_multipoles.shape, F32),
            jax.ShapeDtypeStruct(coarse_multipoles.shape, F32),
        ],
        in_specs=[vmem, hbm, hbm, hbm, hbm],
        out_specs=[vmem, vmem],
        scratch_shapes=[
            pltpu.VMEM(fine_multipoles.shape, BF16),
            pltpu.VMEM(coarse_multipoles.shape, BF16),
            pltpu.VMEM((64, 64, OFFSETS), BF16),
            pltpu.VMEM((64, 64, OFFSETS), BF16),
            pltpu.VMEM((groups * 256, 128), F32),
            pltpu.VMEM((groups, 6, 64, 128), BF16),
            pltpu.VMEM((groups, 6, 64, 128), BF16),
            pltpu.VMEM((4, SLOTS, 16, 128), BF16),
            pltpu.VMEM((3, SLOTS, 16, 128), BF16),
            pltpu.VMEM((2, SLOTS, 16, 128), BF16),
            pltpu.VMEM((2, SLOTS, 16, 128), BF16),
            pltpu.VMEM((128, 128), F32),
            pltpu.VMEM((192, 128), F32),
            pltpu.VMEM((2, 48, 128), F32),
            pltpu.VMEM((2, 48, 128), BF16),
            pltpu.VMEM((2, 48, 128), BF16),
            pltpu.VMEM((2, 48, 128), F32),
            pltpu.VMEM((128, 128), F32),
            pltpu.SemaphoreType.DMA((4,)),
            pltpu.SemaphoreType.DMA((2,)),
            pltpu.SemaphoreType.DMA((2,)),
            pltpu.SemaphoreType.DMA((8,)),
            pltpu.SemaphoreType.DMA((8,)),
        ],
        compiler_params=pltpu.CompilerParams(
            collective_id=0, has_side_effects=True, vmem_limit_bytes=56 * 1024 * 1024
        ),
        name="translate",
    )(
        jnp.asarray(place_selection(), BF16),
        fine_multipoles,
        jnp.transpose(fine_translations, (1, 2, 0)),
        coarse_multipoles,
        jnp.transpose(coarse_translations, (1, 2, 0)),
    )


def solution(mesh):
    sizes = tuple(mesh.shape[axis] for axis in ("gx", "gy", "gz"))
    return jax.shard_map(
        functools.partial(body, sizes),
        mesh=mesh,
        in_specs=(P("gx", "gy", "gz", None), P(), P("gx", "gy", "gz", None), P()),
        out_specs=(P("gx", "gy", "gz", None), P("gx", "gy", "gz", None)),
        check_vma=False,
    )
```

```python
import functools

import jax
import jax.numpy as jnp
import numpy as np
from jax import lax
from jax.experimental import pallas as pl
from jax.experimental.pallas import tpu as pltpu
from jax.sharding import PartitionSpec as P

MESH = pl.DeviceIdType.MESH
BF16 = jnp.bfloat16
F32 = jnp.float32

GROUPS = [(0, ey) for ey in range(4)] + [(ex, ey) for ex in range(1, 4) for ey in range(-3, 4)]
OFFSETS = 158
Y_PAIRS = ((-3, -2), (-1, 0), (1, 2), (3,))
PLANE = [(sx, sz) for sx in (-1, 0, 1) for sz in (-1, 0, 1) if (sx, sz) != (0, 0)]
FINE_SLOTS = (0, 2, 4, 5, 6, 8)
COARSE_SLOTS = (1, 3, 7, 9)
SLOTS = 10
TURN = 8


def group(ex, ey):
    return ey if ex == 0 else 4 + (ex - 1) * 7 + ey + 3


def half_offsets():
    listed = []
    for step_x in range(-3, 4):
        for step_y in range(-3, 4):
            for step_z in range(-3, 4):
                if max(abs(step_x), abs(step_y), abs(step_z)) < 2:
                    continue
                if step_x > 0 or (step_x == 0 and (step_y > 0 or (step_y == 0 and step_z > 0))):
                    listed.append((step_x, step_y, step_z))
    return listed


def place_selection():
    picks = np.zeros((8 * len(GROUPS), OFFSETS), np.float32)
    for index, (x, y, z) in enumerate(half_offsets()):
        picks[8 * group(x, y) + z + 3, index] = 1.0
    return picks


def pack_level(src, stage, own, up, down, nz, base, msg_base):
    zp = nz // 2
    stage[0 : 16 * nz, 0:64] = src[...].astype(F32).reshape(16 * nz, 64)
    for x in range(4):
        for y in range(4):
            row = (x * 4 + y) * nz
            even = stage[pl.ds(row, zp, stride=2), 0:64]
            odd = stage[pl.ds(row + 1, zp, stride=2), 0:64]
            both = jnp.concatenate([even, odd], axis=1)
            tile = (x // 2) * zp * 2 + x % 2
            own[pl.ds(base + tile * 8 + 2 + y, zp, stride=16), :] = both
            face = up if y >= 2 else down
            face[pl.ds(msg_base + tile * 2 + y % 2, zp, stride=4), :] = both


def unpack_level(dst, tiles, nz):
    zp = nz // 2
    for x in range(4):
        for y in range(4):
            start = ((x // 2) * zp * 2 + x % 2) * 8 + y
            both = tiles[pl.ds(start, zp, stride=16), :]
            dst[x, y, pl.ds(0, zp, stride=2), :] = both[:, 0:64]
            dst[x, y, pl.ds(1, zp, stride=2), :] = both[:, 64:128]


def turn_table(picks, table, turned):
    @pl.loop(0, 32 // TURN)
    def _(step):
        for at in range(0, TURN, 2):
            first = step * TURN + at
            rows = jnp.concatenate(
                [table[first], table[32 + first], table[first + 1], table[33 + first]], axis=0
            )
            classes = dot_ahead(picks[...], rows)
            for g in range(len(GROUPS)):
                start = pl.multiple_of(g * 256 + first * 8, 8)
                turned[pl.ds(start, 8), :] = classes[g * 8 : g * 8 + 8, 0:128]
                turned[pl.ds(start + 8, 8), :] = classes[g * 8 : g * 8 + 8, 128:256]


def build_weights(turned, weights):
    left = lax.broadcasted_iota(jnp.int32, (32, 128), 1) < 64

    @pl.loop(0, len(GROUPS) // 5)
    def _(step):
        for at in range(5):
            g = step * 5 + at
            blocks = [turned[pl.ds(g * 256 + e, 32, stride=8), :] for e in range(7)]
            swapped = [pltpu.roll(block, 64, 1) for block in blocks]
            for j in range(6):
                weights[g, j, 0:32] = jnp.where(left, blocks[j], swapped[j + 1]).astype(BF16)
                weights[g, j, 32:64] = jnp.where(left, swapped[j], blocks[j + 1]).astype(BF16)


def ahead(weights, g):
    rows = [jnp.concatenate([weights[g, j + 2 * step] for step in range(3)], axis=1) for j in (1, 0)]
    return jnp.concatenate(rows, axis=0)


def behind(weights, g):
    return jnp.concatenate([weights[g, 5 - s] for s in range(6)], axis=0)


def shift_tiles(halo, odd, high, low):
    zero = jnp.zeros((8, 128), F32)

    @pl.loop(0, SLOTS)
    def _(s):
        wide = [halo[q, s].astype(F32) for q in range(4)]
        for q in range(3):
            odd[q, s] = jnp.concatenate([wide[q][8:16], wide[q + 1][0:8]], axis=0).astype(BF16)
        for q in range(2):
            high[q, s] = jnp.concatenate([wide[q + 2][8:16], zero], axis=0).astype(BF16)
            low[q, s] = jnp.concatenate([zero, wide[q][0:8]], axis=0).astype(BF16)


def sources(halo, odd, high, low, dx, slots):
    if dx % 2 == 0:
        part, first = halo, 1 + dx // 2
    elif dx == 3:
        part, first = high, 0
    elif dx == -3:
        part, first = low, 0
    else:
        part, first = odd, (dx + 1) // 2
    zp = len(slots) - 2
    columns = []
    for step in range(3):
        columns.append(
            jnp.concatenate([part[first + q, slots[z + step]] for q in range(2) for z in range(zp)], axis=0)
        )
    return jnp.concatenate(columns, axis=1)


def dot_ahead(left, weights):
    return lax.dot_general(left, weights, (((1,), (1,)), ((), ())), preferred_element_type=F32)


def dot_behind(left, weights):
    return lax.dot_general(left, weights, (((1,), (0,)), ((), ())), preferred_element_type=F32)


def level(halo, odd, high, low, weights, slots):
    get = functools.partial(sources, halo, odd, high, low, slots=slots)
    forward = {x: get(x) for x in range(0, 4)}
    backward = {x: get(-x) for x in range(0, 4)}
    rows = forward[0].shape[0]
    y = lax.broadcasted_iota(jnp.int32, (rows // 8, 8, 128), 1)
    total = None
    for pair in Y_PAIRS:
        xs = range(0, 4) if min(pair) >= 0 else range(1, 4)
        left = jnp.concatenate([forward[x] for x in xs], axis=1)
        right = jnp.concatenate(
            [jnp.concatenate([ahead(weights, group(x, ey)) for x in xs], axis=1) for ey in pair], axis=0
        )
        sums = dot_ahead(left, right)
        xs = range(0, 4) if max(pair) <= 0 else range(1, 4)
        left = jnp.concatenate([backward[x] for x in xs], axis=1)
        right = jnp.concatenate(
            [jnp.concatenate([behind(weights, group(x, -ey)) for x in xs], axis=0) for ey in pair], axis=1
        )
        sums = sums + dot_behind(left, right)
        for place, ey in enumerate(pair):
            term = sums[:, place * 128 : place * 128 + 128]
            if ey == 0:
                term = term + dot_ahead(forward[0], ahead(weights, group(0, 0)))
            term = term.reshape(rows // 8, 8, 128)
            term = pltpu.roll(term, (-(2 + ey)) % 8, 1)
            if ey == 3:
                term = jnp.where(y % 2 == 0, term, 0.0)
            if ey == -3:
                term = jnp.where(y % 2 == 1, term, 0.0)
            total = term if total is None else total + term
    return total.reshape(rows, 128)


def kernel(
    sizes, picks_hbm, fine_hbm, fine_table_hbm, coarse_hbm, coarse_table_hbm, fine_out, coarse_out,
    picks, fine, coarse, fine_table, coarse_table, turned, fine_weights, coarse_weights,
    halo, odd, high, low, stage, own, faces, sent, got, spread, tiles,
    load_sem, y_send, y_recv, plane_send, plane_recv, ready,
):
    nx, ny, nz = sizes
    gx, gy, gz = lax.axis_index("gx"), lax.axis_index("gy"), lax.axis_index("gz")

    loads = [
        pltpu.make_async_copy(src, dst, load_sem.at[k])
        for k, (src, dst) in enumerate((
            (fine_hbm, fine), (coarse_hbm, coarse), (picks_hbm, picks),
            (fine_table_hbm, fine_table), (coarse_table_hbm, coarse_table),
        ))
    ]
    for load in loads:
        load.start()

    def in_y(sy):
        return (gy + sy >= 0) & (gy + sy < ny)

    def in_plane(sx, sz):
        return (gx + sx >= 0) & (gx + sx < nx) & (gz + sz >= 0) & (gz + sz < nz)

    def at_y(sy):
        return (gx, lax.rem(gy + sy + ny, ny), gz)

    def at_plane(sx, sz):
        return (lax.rem(gx + sx + nx, nx), gy, lax.rem(gz + sz + nz, nz))

    phase = lax.rem(gy, 4)
    waits = {1: phase >= 2, -1: (phase == 1) | (phase == 2)}
    barrier = pltpu.get_barrier_semaphore()
    greetings = jnp.int32(0)
    for sy in (1, -1):
        greetings += (in_y(sy) & waits[sy]).astype(jnp.int32)

        @pl.when(in_y(sy) & jnp.logical_not(waits[sy]))
        def _():
            pl.semaphore_signal(barrier, inc=1, device_id=at_y(sy), device_id_type=MESH)

    for sx, sz in PLANE:
        greetings += in_plane(sx, sz).astype(jnp.int32)

        @pl.when(in_plane(sx, sz))
        def _():
            pl.semaphore_signal(barrier, inc=1, device_id=at_plane(sx, sz), device_id_type=MESH)

    loads[0].wait()
    loads[1].wait()
    pack_level(fine, stage, own, faces.at[0], faces.at[1], 8, 0, 0)
    pack_level(coarse, stage, own, faces.at[0], faces.at[1], 4, 128, 32)
    sent[...] = faces[...].astype(BF16)

    y_copies = [
        (sy, pltpu.make_async_remote_copy(
            src_ref=sent.at[k], dst_ref=got.at[k], send_sem=y_send.at[k], recv_sem=y_recv.at[k],
            device_id=at_y(sy), device_id_type=MESH,
        ))
        for k, sy in enumerate((1, -1))
    ]
    pl.semaphore_wait(barrier, greetings)
    for k, (sy, copy) in enumerate(y_copies):

        @pl.when(in_y(sy) & waits[sy])
        def _():
            copy.start()
            pl.semaphore_signal(ready.at[1 - k], inc=1, device_id=at_y(sy), device_id_type=MESH)

    @pl.when(gx == 0)
    def _():
        halo[0] = jnp.zeros((SLOTS, 16, 128), BF16)

    @pl.when(gx == nx - 1)
    def _():
        halo[3] = jnp.zeros((SLOTS, 16, 128), BF16)

    @pl.when(gz == 0)
    def _():
        halo[:, 0:2] = jnp.zeros((4, 2, 16, 128), BF16)

    @pl.when(gz == nz - 1)
    def _():
        halo[:, 8:10] = jnp.zeros((4, 2, 16, 128), BF16)

    @pl.when(gy == 0)
    def _():
        got[0] = jnp.zeros((48, 128), BF16)

    @pl.when(gy == ny - 1)
    def _():
        got[1] = jnp.zeros((48, 128), BF16)

    loads[2].wait()
    loads[3].wait()
    turn_table(picks, fine_table, turned)
    build_weights(turned, fine_weights)
    loads[4].wait()
    turn_table(picks, coarse_table, turned)
    build_weights(turned, coarse_weights)

    for k, (sy, copy) in enumerate(y_copies):

        @pl.when(in_y(sy) & jnp.logical_not(waits[sy]))
        def _():
            pl.semaphore_wait(ready.at[k], 1)
            copy.start()

    for sy, copy in y_copies:

        @pl.when(in_y(-sy))
        def _():
            copy.wait_recv()

    spread[...] = got[...].astype(F32)
    for row in range(2):
        own[pl.ds(row, 24, stride=8), :] = spread[0, pl.ds(row, 24, stride=2), :]
        own[pl.ds(6 + row, 24, stride=8), :] = spread[1, pl.ds(row, 24, stride=2), :]
    for q in range(2):
        for slots, zp, base in ((FINE_SLOTS, 4, 0), (COARSE_SLOTS, 2, 128)):
            for z in range(zp):
                start = base + (q * zp + z) * 16
                halo[1 + q, slots[1 + z]] = own[start : start + 16, :].astype(BF16)

    plane_copies = []
    for k, (sx, sz) in enumerate(PLANE):
        x_from, x_to, x_count = {-1: (1, 3, 1), 0: (1, 1, 2), 1: (2, 0, 1)}[sx]
        z_from, z_to, z_count = {-1: (2, 8, 2), 0: (2, 2, 6), 1: (6, 0, 2)}[sz]
        plane_copies.append((
            sx, sz, pltpu.make_async_remote_copy(
                src_ref=halo.at[pl.ds(x_from, x_count), pl.ds(z_from, z_count)],
                dst_ref=halo.at[pl.ds(x_to, x_count), pl.ds(z_to, z_count)],
                send_sem=plane_send.at[k], recv_sem=plane_recv.at[k],
                device_id=at_plane(sx, sz), device_id_type=MESH,
            )
        ))
    for sx, sz, copy in plane_copies:

        @pl.when(in_plane(sx, sz))
        def _():
            copy.start()

    for sx, sz, copy in plane_copies:

        @pl.when(in_plane(-sx, -sz))
        def _():
            copy.wait_recv()

    shift_tiles(halo, odd, high, low)
    tiles[...] = level(halo, odd, high, low, fine_weights, FINE_SLOTS)
    unpack_level(fine_out, tiles, 8)
    tiles[0:64, :] = level(halo, odd, high, low, coarse_weights, COARSE_SLOTS)
    unpack_level(coarse_out, tiles, 4)

    for sy, copy in y_copies:

        @pl.when(in_y(sy))
        def _():
            copy.wait_send()

    for sx, sz, copy in plane_copies:

        @pl.when(in_plane(sx, sz))
        def _():
            copy.wait_send()


def body(sizes, fine_multipoles, fine_translations, coarse_multipoles, coarse_translations):
    vmem = pl.BlockSpec(memory_space=pltpu.VMEM)
    hbm = pl.BlockSpec(memory_space=pl.ANY)
    groups = len(GROUPS)
    return pl.pallas_call(
        functools.partial(kernel, sizes),
        out_shape=[
            pltpu.VMEM(fine_multipoles.shape, F32),
            pltpu.VMEM(coarse_multipoles.shape, F32),
        ],
        in_specs=[hbm] * 5,
        out_specs=[vmem, vmem],
        scratch_shapes=[
            pltpu.VMEM((8 * groups, OFFSETS), BF16),
            pltpu.VMEM(fine_multipoles.shape, BF16),
            pltpu.VMEM(coarse_multipoles.shape, BF16),
            pltpu.VMEM((64, 64, OFFSETS), BF16),
            pltpu.VMEM((64, 64, OFFSETS), BF16),
            pltpu.VMEM((groups * 256, 128), F32),
            pltpu.VMEM((groups, 6, 64, 128), BF16),
            pltpu.VMEM((groups, 6, 64, 128), BF16),
            pltpu.VMEM((4, SLOTS, 16, 128), BF16),
            pltpu.VMEM((3, SLOTS, 16, 128), BF16),
            pltpu.VMEM((2, SLOTS, 16, 128), BF16),
            pltpu.VMEM((2, SLOTS, 16, 128), BF16),
            pltpu.VMEM((128, 128), F32),
            pltpu.VMEM((192, 128), F32),
            pltpu.VMEM((2, 48, 128), F32),
            pltpu.VMEM((2, 48, 128), BF16),
            pltpu.VMEM((2, 48, 128), BF16),
            pltpu.VMEM((2, 48, 128), F32),
            pltpu.VMEM((128, 128), F32),
            pltpu.SemaphoreType.DMA((5,)),
            pltpu.SemaphoreType.DMA((2,)),
            pltpu.SemaphoreType.DMA((2,)),
            pltpu.SemaphoreType.DMA((8,)),
            pltpu.SemaphoreType.DMA((8,)),
            pltpu.SemaphoreType.REGULAR((2,)),
        ],
        compiler_params=pltpu.CompilerParams(
            collective_id=0, has_side_effects=True, vmem_limit_bytes=24 * 1024 * 1024
        ),
        name="translate",
    )(*(
        pltpu.with_memory_space_constraint(array, pltpu.HBM)
        for array in (
            jnp.asarray(place_selection(), BF16),
            fine_multipoles,
            jnp.transpose(fine_translations, (1, 2, 0)),
            coarse_multipoles,
            jnp.transpose(coarse_translations, (1, 2, 0)),
        )
    ))


def solution(mesh):
    sizes = tuple(mesh.shape[axis] for axis in ("gx", "gy", "gz"))
    return jax.shard_map(
        functools.partial(body, sizes),
        mesh=mesh,
        in_specs=(P("gx", "gy", "gz", None), P(), P("gx", "gy", "gz", None), P()),
        out_specs=(P("gx", "gy", "gz", None), P("gx", "gy", "gz", None)),
        check_vma=False,
    )
```

```python
import functools

import jax
import jax.numpy as jnp
import numpy as np
from jax import lax
from jax.experimental import pallas as pl
from jax.experimental.pallas import tpu as pltpu
from jax.sharding import PartitionSpec as P

MESH = pl.DeviceIdType.MESH
BF16 = jnp.bfloat16
F32 = jnp.float32

GROUPS = [(0, ey) for ey in range(4)] + [(ex, ey) for ex in range(1, 4) for ey in range(-3, 4)]
OFFSETS = 158
Y_PAIRS = ((-3, -2), (-1, 0), (1, 2), (3,))
PLANE = [(-1, -1), (-1, 1), (1, -1), (1, 1), (0, -1), (0, 1), (-1, 0), (1, 0)]
FINE_SLOTS = (0, 2, 4, 5, 6, 8)
COARSE_SLOTS = (1, 3, 7, 9)
SLOTS = 10
TURN = 8


def group(ex, ey):
    return ey if ex == 0 else 4 + (ex - 1) * 7 + ey + 3


def half_offsets():
    listed = []
    for step_x in range(-3, 4):
        for step_y in range(-3, 4):
            for step_z in range(-3, 4):
                if max(abs(step_x), abs(step_y), abs(step_z)) < 2:
                    continue
                if step_x > 0 or (step_x == 0 and (step_y > 0 or (step_y == 0 and step_z > 0))):
                    listed.append((step_x, step_y, step_z))
    return listed


def place_selection():
    picks = np.zeros((8 * len(GROUPS), OFFSETS), np.float32)
    for index, (x, y, z) in enumerate(half_offsets()):
        picks[8 * group(x, y) + z + 3, index] = 1.0
    return picks


def pack_level(src, stage, own, up, down, nz, base, msg_base):
    zp = nz // 2
    stage[0 : 16 * nz, 0:64] = src[...].astype(F32).reshape(16 * nz, 64)
    for x in range(4):
        for y in range(4):
            row = (x * 4 + y) * nz
            even = stage[pl.ds(row, zp, stride=2), 0:64]
            odd = stage[pl.ds(row + 1, zp, stride=2), 0:64]
            both = jnp.concatenate([even, odd], axis=1)
            tile = (x // 2) * zp * 2 + x % 2
            own[pl.ds(base + tile * 8 + 2 + y, zp, stride=16), :] = both
            face = up if y >= 2 else down
            face[pl.ds(msg_base + tile * 2 + y % 2, zp, stride=4), :] = both


def unpack_level(dst, tiles, nz, base):
    zp = nz // 2
    for x in range(4):
        for y in range(4):
            start = base + ((x // 2) * zp * 2 + x % 2) * 8 + y
            both = tiles[pl.ds(start, zp, stride=16), :]
            dst[x, y, pl.ds(0, zp, stride=2), :] = both[:, 0:64]
            dst[x, y, pl.ds(1, zp, stride=2), :] = both[:, 64:128]


def turn_table(picks, table, turned):
    @pl.loop(0, 32 // TURN)
    def _(step):
        for at in range(0, TURN, 2):
            first = step * TURN + at
            rows = jnp.concatenate(
                [table[first], table[32 + first], table[first + 1], table[33 + first]], axis=0
            )
            classes = dot_ahead(picks[...], rows)
            for g in range(len(GROUPS)):
                start = pl.multiple_of(g * 256 + first * 8, 8)
                turned[pl.ds(start, 8), :] = classes[g * 8 : g * 8 + 8, 0:128]
                turned[pl.ds(start + 8, 8), :] = classes[g * 8 : g * 8 + 8, 128:256]


def build_weights(turned, weights):
    left = lax.broadcasted_iota(jnp.int32, (32, 128), 1) < 64

    @pl.loop(0, len(GROUPS) // 5)
    def _(step):
        for at in range(5):
            g = step * 5 + at
            blocks = [turned[pl.ds(g * 256 + e, 32, stride=8), :] for e in range(7)]
            swapped = [pltpu.roll(block, 64, 1) for block in blocks]
            for j in range(6):
                weights[g, j, 0:32] = jnp.where(left, blocks[j], swapped[j + 1]).astype(BF16)
                weights[g, j, 32:64] = jnp.where(left, swapped[j], blocks[j + 1]).astype(BF16)


def ahead(weights, g):
    rows = [jnp.concatenate([weights[g, j + 2 * step] for step in range(3)], axis=1) for j in (1, 0)]
    return jnp.concatenate(rows, axis=0)


def behind(weights, g):
    return jnp.concatenate([weights[g, 5 - s] for s in range(6)], axis=0)


def shift_tiles(halo, odd, high, low):
    zero = jnp.zeros((8, 128), F32)

    @pl.loop(0, SLOTS)
    def _(s):
        wide = [halo[q, s].astype(F32) for q in range(4)]
        for q in range(3):
            odd[q, s] = jnp.concatenate([wide[q][8:16], wide[q + 1][0:8]], axis=0).astype(BF16)
        for q in range(2):
            high[q, s] = jnp.concatenate([wide[q + 2][8:16], zero], axis=0).astype(BF16)
            low[q, s] = jnp.concatenate([zero, wide[q][0:8]], axis=0).astype(BF16)


def sources(halo, odd, high, low, dx, slots):
    if dx % 2 == 0:
        part, first = halo, 1 + dx // 2
    elif dx == 3:
        part, first = high, 0
    elif dx == -3:
        part, first = low, 0
    else:
        part, first = odd, (dx + 1) // 2
    zp = len(slots) - 2
    columns = []
    for step in range(3):
        columns.append(
            jnp.concatenate([part[first + q, slots[z + step]] for q in range(2) for z in range(zp)], axis=0)
        )
    return jnp.concatenate(columns, axis=1)


def dot_ahead(left, weights):
    return lax.dot_general(left, weights, (((1,), (1,)), ((), ())), preferred_element_type=F32)


def dot_behind(left, weights):
    return lax.dot_general(left, weights, (((1,), (0,)), ((), ())), preferred_element_type=F32)


def level(halo, odd, high, low, weights, slots):
    get = functools.partial(sources, halo, odd, high, low, slots=slots)
    forward = {x: get(x) for x in range(0, 4)}
    backward = {x: get(-x) for x in range(0, 4)}
    rows = forward[0].shape[0]
    y = lax.broadcasted_iota(jnp.int32, (rows // 8, 8, 128), 1)
    total = None
    for pair in Y_PAIRS:
        xs = range(0, 4) if min(pair) >= 0 else range(1, 4)
        left = jnp.concatenate([forward[x] for x in xs], axis=1)
        right = jnp.concatenate(
            [jnp.concatenate([ahead(weights, group(x, ey)) for x in xs], axis=1) for ey in pair], axis=0
        )
        sums = dot_ahead(left, right)
        xs = range(0, 4) if max(pair) <= 0 else range(1, 4)
        left = jnp.concatenate([backward[x] for x in xs], axis=1)
        right = jnp.concatenate(
            [jnp.concatenate([behind(weights, group(x, -ey)) for x in xs], axis=0) for ey in pair], axis=1
        )
        sums = sums + dot_behind(left, right)
        for place, ey in enumerate(pair):
            term = sums[:, place * 128 : place * 128 + 128]
            if ey == 0:
                term = term + dot_ahead(forward[0], ahead(weights, group(0, 0)))
            term = term.reshape(rows // 8, 8, 128)
            term = pltpu.roll(term, (-(2 + ey)) % 8, 1)
            if ey == 3:
                term = jnp.where(y % 2 == 0, term, 0.0)
            if ey == -3:
                term = jnp.where(y % 2 == 1, term, 0.0)
            total = term if total is None else total + term
    return total.reshape(rows, 128)


def kernel(
    sizes, picks_hbm, fine_hbm, fine_table_hbm, coarse_hbm, coarse_table_hbm, tiles,
    picks, fine, coarse, fine_table, coarse_table, turned, fine_weights, coarse_weights,
    halo, odd, high, low, stage, own, faces, sent, got, spread,
    load_sem, y_send, y_recv, plane_send, plane_recv, ready,
):
    nx, ny, nz = sizes
    gx, gy, gz = lax.axis_index("gx"), lax.axis_index("gy"), lax.axis_index("gz")

    loads = [
        pltpu.make_async_copy(src, dst, load_sem.at[k])
        for k, (src, dst) in enumerate((
            (fine_hbm, fine), (coarse_hbm, coarse), (picks_hbm, picks),
            (fine_table_hbm, fine_table), (coarse_table_hbm, coarse_table),
        ))
    ]
    for load in loads:
        load.start()

    def in_y(sy):
        return (gy + sy >= 0) & (gy + sy < ny)

    def in_plane(sx, sz):
        return (gx + sx >= 0) & (gx + sx < nx) & (gz + sz >= 0) & (gz + sz < nz)

    def at_y(sy):
        return (gx, lax.rem(gy + sy + ny, ny), gz)

    def at_plane(sx, sz):
        return (lax.rem(gx + sx + nx, nx), gy, lax.rem(gz + sz + nz, nz))

    phase = lax.rem(gy, 4)
    waits = {1: phase >= 2, -1: (phase == 1) | (phase == 2)}
    barrier = pltpu.get_barrier_semaphore()
    greetings = jnp.int32(0)
    for sy in (1, -1):
        greetings += (in_y(sy) & waits[sy]).astype(jnp.int32)

        @pl.when(in_y(sy) & jnp.logical_not(waits[sy]))
        def _():
            pl.semaphore_signal(barrier, inc=1, device_id=at_y(sy), device_id_type=MESH)

    for sx, sz in PLANE:
        greetings += in_plane(sx, sz).astype(jnp.int32)

        @pl.when(in_plane(sx, sz))
        def _():
            pl.semaphore_signal(barrier, inc=1, device_id=at_plane(sx, sz), device_id_type=MESH)

    loads[0].wait()
    loads[1].wait()
    pack_level(fine, stage, own, faces.at[0], faces.at[1], 8, 0, 0)
    pack_level(coarse, stage, own, faces.at[0], faces.at[1], 4, 128, 32)
    sent[...] = faces[...].astype(BF16)

    y_copies = [
        (sy, pltpu.make_async_remote_copy(
            src_ref=sent.at[k], dst_ref=got.at[k], send_sem=y_send.at[k], recv_sem=y_recv.at[k],
            device_id=at_y(sy), device_id_type=MESH,
        ))
        for k, sy in enumerate((1, -1))
    ]
    pl.semaphore_wait(barrier, greetings)
    for k, (sy, copy) in enumerate(y_copies):

        @pl.when(in_y(sy) & waits[sy])
        def _():
            copy.start()
            pl.semaphore_signal(ready.at[1 - k], inc=1, device_id=at_y(sy), device_id_type=MESH)

    @pl.when(gx == 0)
    def _():
        halo[0] = jnp.zeros((SLOTS, 16, 128), BF16)

    @pl.when(gx == nx - 1)
    def _():
        halo[3] = jnp.zeros((SLOTS, 16, 128), BF16)

    @pl.when(gz == 0)
    def _():
        halo[:, 0:2] = jnp.zeros((4, 2, 16, 128), BF16)

    @pl.when(gz == nz - 1)
    def _():
        halo[:, 8:10] = jnp.zeros((4, 2, 16, 128), BF16)

    @pl.when(gy == 0)
    def _():
        got[0] = jnp.zeros((48, 128), BF16)

    @pl.when(gy == ny - 1)
    def _():
        got[1] = jnp.zeros((48, 128), BF16)

    loads[2].wait()
    loads[3].wait()
    turn_table(picks, fine_table, turned)
    build_weights(turned, fine_weights)
    loads[4].wait()
    turn_table(picks, coarse_table, turned)
    build_weights(turned, coarse_weights)

    for k, (sy, copy) in enumerate(y_copies):

        @pl.when(in_y(sy) & jnp.logical_not(waits[sy]))
        def _():
            pl.semaphore_wait(ready.at[k], 1)
            copy.start()

    for sy, copy in y_copies:

        @pl.when(in_y(-sy))
        def _():
            copy.wait_recv()

    spread[...] = got[...].astype(F32)
    for row in range(2):
        own[pl.ds(row, 24, stride=8), :] = spread[0, pl.ds(row, 24, stride=2), :]
        own[pl.ds(6 + row, 24, stride=8), :] = spread[1, pl.ds(row, 24, stride=2), :]
    for q in range(2):
        for slots, zp, base in ((FINE_SLOTS, 4, 0), (COARSE_SLOTS, 2, 128)):
            for z in range(zp):
                start = base + (q * zp + z) * 16
                halo[1 + q, slots[1 + z]] = own[start : start + 16, :].astype(BF16)

    plane_copies = []
    for k, (sx, sz) in enumerate(PLANE):
        x_from, x_to, x_count = {-1: (1, 3, 1), 0: (1, 1, 2), 1: (2, 0, 1)}[sx]
        z_from, z_to, z_count = {-1: (2, 8, 2), 0: (2, 2, 6), 1: (6, 0, 2)}[sz]
        plane_copies.append((
            sx, sz, pltpu.make_async_remote_copy(
                src_ref=halo.at[pl.ds(x_from, x_count), pl.ds(z_from, z_count)],
                dst_ref=halo.at[pl.ds(x_to, x_count), pl.ds(z_to, z_count)],
                send_sem=plane_send.at[k], recv_sem=plane_recv.at[k],
                device_id=at_plane(sx, sz), device_id_type=MESH,
            )
        ))
    for sx, sz, copy in plane_copies:

        @pl.when(in_plane(sx, sz))
        def _():
            copy.start()

    for sx, sz, copy in plane_copies:

        @pl.when(in_plane(-sx, -sz))
        def _():
            copy.wait_recv()

    shift_tiles(halo, odd, high, low)
    tiles[0:128, :] = level(halo, odd, high, low, fine_weights, FINE_SLOTS)
    tiles[128:192, :] = level(halo, odd, high, low, coarse_weights, COARSE_SLOTS)

    for sy, copy in y_copies:

        @pl.when(in_y(sy))
        def _():
            copy.wait_send()

    for sx, sz, copy in plane_copies:

        @pl.when(in_plane(sx, sz))
        def _():
            copy.wait_send()


def place(tiles, fine_out, coarse_out):
    unpack_level(fine_out, tiles, 8, 0)
    unpack_level(coarse_out, tiles, 4, 128)


def body(sizes, fine_multipoles, fine_translations, coarse_multipoles, coarse_translations):
    vmem = pl.BlockSpec(memory_space=pltpu.VMEM)
    hbm = pl.BlockSpec(memory_space=pl.ANY)
    groups = len(GROUPS)
    tiles = pl.pallas_call(
        functools.partial(kernel, sizes),
        out_shape=pltpu.VMEM((192, 128), F32),
        in_specs=[hbm] * 5,
        out_specs=vmem,
        scratch_shapes=[
            pltpu.VMEM((8 * groups, OFFSETS), BF16),
            pltpu.VMEM(fine_multipoles.shape, BF16),
            pltpu.VMEM(coarse_multipoles.shape, BF16),
            pltpu.VMEM((64, 64, OFFSETS), BF16),
            pltpu.VMEM((64, 64, OFFSETS), BF16),
            pltpu.VMEM((groups * 256, 128), F32),
            pltpu.VMEM((groups, 6, 64, 128), BF16),
            pltpu.VMEM((groups, 6, 64, 128), BF16),
            pltpu.VMEM((4, SLOTS, 16, 128), BF16),
            pltpu.VMEM((3, SLOTS, 16, 128), BF16),
            pltpu.VMEM((2, SLOTS, 16, 128), BF16),
            pltpu.VMEM((2, SLOTS, 16, 128), BF16),
            pltpu.VMEM((128, 128), F32),
            pltpu.VMEM((192, 128), F32),
            pltpu.VMEM((2, 48, 128), F32),
            pltpu.VMEM((2, 48, 128), BF16),
            pltpu.VMEM((2, 48, 128), BF16),
            pltpu.VMEM((2, 48, 128), F32),
            pltpu.SemaphoreType.DMA((5,)),
            pltpu.SemaphoreType.DMA((2,)),
            pltpu.SemaphoreType.DMA((2,)),
            pltpu.SemaphoreType.DMA((8,)),
            pltpu.SemaphoreType.DMA((8,)),
            pltpu.SemaphoreType.REGULAR((2,)),
        ],
        compiler_params=pltpu.CompilerParams(
            collective_id=0, has_side_effects=True, vmem_limit_bytes=24 * 1024 * 1024
        ),
        name="translate",
    )(*(
        pltpu.with_memory_space_constraint(array, pltpu.HBM)
        for array in (
            jnp.asarray(place_selection(), BF16),
            fine_multipoles,
            jnp.transpose(fine_translations, (1, 2, 0)),
            coarse_multipoles,
            jnp.transpose(coarse_translations, (1, 2, 0)),
        )
    ))
    return pl.pallas_call(
        place,
        out_shape=[
            jax.ShapeDtypeStruct(fine_multipoles.shape, F32),
            jax.ShapeDtypeStruct(coarse_multipoles.shape, F32),
        ],
        in_specs=[vmem],
        out_specs=[vmem, vmem],
        name="place",
    )(pltpu.with_memory_space_constraint(tiles, pltpu.VMEM))


def solution(mesh):
    sizes = tuple(mesh.shape[axis] for axis in ("gx", "gy", "gz"))
    return jax.shard_map(
        functools.partial(body, sizes),
        mesh=mesh,
        in_specs=(P("gx", "gy", "gz", None), P(), P("gx", "gy", "gz", None), P()),
        out_specs=(P("gx", "gy", "gz", None), P("gx", "gy", "gz", None)),
        check_vma=False,
    )
```

```python
import functools

import jax
import jax.numpy as jnp
import numpy as np
from jax import lax
from jax.experimental import pallas as pl
from jax.experimental.pallas import tpu as pltpu
from jax.sharding import PartitionSpec as P

MESH = pl.DeviceIdType.MESH
BF16 = jnp.bfloat16
F32 = jnp.float32

GROUPS = [(0, ey) for ey in range(4)] + [(ex, ey) for ex in range(1, 4) for ey in range(-3, 4)]
OFFSETS = 158
OWN, BELOW, ABOVE = range(3)
Y_PAIRS = (((-3, -2), (-1, 0), (1, 2), (3,)), ((-3, -2), (-1,)), ((1, 2), (3,)))
PLANE = [(-1, -1), (-1, 1), (1, -1), (1, 1), (0, -1), (0, 1), (-1, 0), (1, 0)]
FINE_SLOTS = (0, 2, 4, 5, 6, 8)
COARSE_SLOTS = (1, 3, 7, 9)
SLOTS = 10
TURN = 8


def group(ex, ey):
    return ey if ex == 0 else 4 + (ex - 1) * 7 + ey + 3


def half_offsets():
    listed = []
    for step_x in range(-3, 4):
        for step_y in range(-3, 4):
            for step_z in range(-3, 4):
                if max(abs(step_x), abs(step_y), abs(step_z)) < 2:
                    continue
                if step_x > 0 or (step_x == 0 and (step_y > 0 or (step_y == 0 and step_z > 0))):
                    listed.append((step_x, step_y, step_z))
    return listed


def place_selection():
    picks = np.zeros((8 * len(GROUPS), OFFSETS), np.float32)
    for index, (x, y, z) in enumerate(half_offsets()):
        picks[8 * group(x, y) + z + 3, index] = 1.0
    return picks


def pack_level(src, stage, own, up, down, nz, base, msg_base):
    zp = nz // 2
    stage[0 : 16 * nz, 0:64] = src[...].astype(F32).reshape(16 * nz, 64)
    for x in range(4):
        for y in range(4):
            row = (x * 4 + y) * nz
            even = stage[pl.ds(row, zp, stride=2), 0:64]
            odd = stage[pl.ds(row + 1, zp, stride=2), 0:64]
            both = jnp.concatenate([even, odd], axis=1)
            tile = (x // 2) * zp * 2 + x % 2
            own[pl.ds(base + tile * 8 + 2 + y, zp, stride=16), :] = both
            face = up if y >= 2 else down
            face[pl.ds(msg_base + tile * 2 + y % 2, zp, stride=4), :] = both


def unpack_level(dst, tiles, nz, base):
    zp = nz // 2
    for x in range(4):
        for y in range(4):
            start = base + ((x // 2) * zp * 2 + x % 2) * 8 + y
            both = tiles[pl.ds(start, zp, stride=16), :]
            dst[x, y, pl.ds(0, zp, stride=2), :] = both[:, 0:64]
            dst[x, y, pl.ds(1, zp, stride=2), :] = both[:, 64:128]


def turn_table(picks, table, turned):
    @pl.loop(0, 32 // TURN)
    def _(step):
        for at in range(0, TURN, 2):
            first = step * TURN + at
            rows = jnp.concatenate(
                [table[first], table[32 + first], table[first + 1], table[33 + first]], axis=0
            )
            classes = dot_ahead(picks[...], rows)
            for g in range(len(GROUPS)):
                start = pl.multiple_of(g * 256 + first * 8, 8)
                turned[pl.ds(start, 8), :] = classes[g * 8 : g * 8 + 8, 0:128]
                turned[pl.ds(start + 8, 8), :] = classes[g * 8 : g * 8 + 8, 128:256]


def build_weights(turned, weights):
    left = lax.broadcasted_iota(jnp.int32, (32, 128), 1) < 64

    @pl.loop(0, len(GROUPS) // 5)
    def _(step):
        for at in range(5):
            g = step * 5 + at
            blocks = [turned[pl.ds(g * 256 + e, 32, stride=8), :] for e in range(7)]
            swapped = [pltpu.roll(block, 64, 1) for block in blocks]
            for j in range(6):
                weights[g, j, 0:32] = jnp.where(left, blocks[j], swapped[j + 1]).astype(BF16)
                weights[g, j, 32:64] = jnp.where(left, swapped[j], blocks[j + 1]).astype(BF16)


def ahead(weights, g):
    rows = [jnp.concatenate([weights[g, j + 2 * step] for step in range(3)], axis=1) for j in (1, 0)]
    return jnp.concatenate(rows, axis=0)


def behind(weights, g):
    return jnp.concatenate([weights[g, 5 - s] for s in range(6)], axis=0)


def shift_tiles(halo, odd, high, low):
    zero = jnp.zeros((8, 128), F32)

    @pl.loop(0, SLOTS)
    def _(s):
        wide = [halo[q, s].astype(F32) for q in range(4)]
        for q in range(3):
            odd[q, s] = jnp.concatenate([wide[q][8:16], wide[q + 1][0:8]], axis=0).astype(BF16)
        for q in range(2):
            high[q, s] = jnp.concatenate([wide[q + 2][8:16], zero], axis=0).astype(BF16)
            low[q, s] = jnp.concatenate([zero, wide[q][0:8]], axis=0).astype(BF16)


def sources(halo, odd, high, low, dx, slots):
    if dx % 2 == 0:
        part, first = halo, 1 + dx // 2
    elif dx == 3:
        part, first = high, 0
    elif dx == -3:
        part, first = low, 0
    else:
        part, first = odd, (dx + 1) // 2
    zp = len(slots) - 2
    columns = []
    for step in range(3):
        columns.append(
            jnp.concatenate([part[first + q, slots[z + step]] for q in range(2) for z in range(zp)], axis=0)
        )
    return jnp.concatenate(columns, axis=1)


def dot_ahead(left, weights):
    return lax.dot_general(left, weights, (((1,), (1,)), ((), ())), preferred_element_type=F32)


def dot_behind(left, weights):
    return lax.dot_general(left, weights, (((1,), (0,)), ((), ())), preferred_element_type=F32)


def level(halo, odd, high, low, weights, slots, slab):
    get = functools.partial(sources, halo, odd, high, low, slots=slots)
    forward = {x: get(x) for x in range(0, 4)}
    backward = {x: get(-x) for x in range(0, 4)}
    rows = forward[0].shape[0]
    y = lax.broadcasted_iota(jnp.int32, (rows // 8, 8, 128), 1)
    total = None
    for pair in Y_PAIRS[slab]:
        xs = range(0, 4) if min(pair) >= 0 else range(1, 4)
        left = jnp.concatenate([forward[x] for x in xs], axis=1)
        right = jnp.concatenate(
            [jnp.concatenate([ahead(weights, group(x, ey)) for x in xs], axis=1) for ey in pair], axis=0
        )
        sums = dot_ahead(left, right)
        xs = range(0, 4) if max(pair) <= 0 else range(1, 4)
        left = jnp.concatenate([backward[x] for x in xs], axis=1)
        right = jnp.concatenate(
            [jnp.concatenate([behind(weights, group(x, -ey)) for x in xs], axis=0) for ey in pair], axis=1
        )
        sums = sums + dot_behind(left, right)
        for place, ey in enumerate(pair):
            term = sums[:, place * 128 : place * 128 + 128]
            if ey == 0:
                term = term + dot_ahead(forward[0], ahead(weights, group(0, 0)))
            term = term.reshape(rows // 8, 8, 128)
            term = pltpu.roll(term, (-(2 + ey)) % 8, 1)
            if ey == 3:
                term = jnp.where(y % 2 == 0, term, 0.0)
            if ey == -3:
                term = jnp.where(y % 2 == 1, term, 0.0)
            total = term if total is None else total + term
    return total.reshape(rows, 128)


def kernel(
    sizes, picks_hbm, fine_hbm, fine_table_hbm, coarse_hbm, coarse_table_hbm, tiles,
    picks, fine, coarse, fine_table, coarse_table, turned, fine_weights, coarse_weights,
    halo, odd, high, low, stage, own, faces, sent, got, spread,
    load_sem, y_send, y_recv, plane_send, plane_recv, ready,
):
    nx, ny, nz = sizes
    gx, gy, gz = lax.axis_index("gx"), lax.axis_index("gy"), lax.axis_index("gz")

    loads = [
        pltpu.make_async_copy(src, dst, load_sem.at[k])
        for k, (src, dst) in enumerate((
            (fine_hbm, fine), (coarse_hbm, coarse), (picks_hbm, picks),
            (fine_table_hbm, fine_table), (coarse_table_hbm, coarse_table),
        ))
    ]
    for load in loads:
        load.start()

    def in_y(sy):
        return (gy + sy >= 0) & (gy + sy < ny)

    def in_plane(sx, sz):
        return (gx + sx >= 0) & (gx + sx < nx) & (gz + sz >= 0) & (gz + sz < nz)

    def at_y(sy):
        return (gx, lax.rem(gy + sy + ny, ny), gz)

    def at_plane(sx, sz):
        return (lax.rem(gx + sx + nx, nx), gy, lax.rem(gz + sz + nz, nz))

    phase = lax.rem(gy, 4)
    waits = {1: phase >= 2, -1: (phase == 1) | (phase == 2)}
    barrier = pltpu.get_barrier_semaphore()
    greetings = jnp.int32(0)
    for sy in (1, -1):
        greetings += (in_y(sy) & waits[sy]).astype(jnp.int32)

        @pl.when(in_y(sy) & jnp.logical_not(waits[sy]))
        def _():
            pl.semaphore_signal(barrier, inc=1, device_id=at_y(sy), device_id_type=MESH)

    for sx, sz in PLANE:
        greetings += in_plane(sx, sz).astype(jnp.int32)

        @pl.when(in_plane(sx, sz))
        def _():
            pl.semaphore_signal(barrier, inc=1, device_id=at_plane(sx, sz), device_id_type=MESH)

    loads[0].wait()
    loads[1].wait()
    own[...] = jnp.zeros((3, 192, 128), F32)
    pack_level(fine, stage, own.at[OWN], faces.at[0], faces.at[1], 8, 0, 0)
    pack_level(coarse, stage, own.at[OWN], faces.at[0], faces.at[1], 4, 128, 32)
    sent[...] = faces[...].astype(BF16)

    y_copies = [
        (sy, pltpu.make_async_remote_copy(
            src_ref=sent.at[k], dst_ref=got.at[k], send_sem=y_send.at[k], recv_sem=y_recv.at[k],
            device_id=at_y(sy), device_id_type=MESH,
        ))
        for k, sy in enumerate((1, -1))
    ]
    pl.semaphore_wait(barrier, greetings)
    for k, (sy, copy) in enumerate(y_copies):

        @pl.when(in_y(sy) & waits[sy])
        def _():
            copy.start()
            pl.semaphore_signal(ready.at[1 - k], inc=1, device_id=at_y(sy), device_id_type=MESH)

    def plane_copies(slab):
        made = []
        for k, (sx, sz) in enumerate(PLANE):
            x_from, x_to, x_count = {-1: (1, 3, 1), 0: (1, 1, 2), 1: (2, 0, 1)}[sx]
            z_from, z_to, z_count = {-1: (2, 8, 2), 0: (2, 2, 6), 1: (6, 0, 2)}[sz]
            made.append((
                sx, sz, pltpu.make_async_remote_copy(
                    src_ref=halo.at[slab, pl.ds(x_from, x_count), pl.ds(z_from, z_count)],
                    dst_ref=halo.at[slab, pl.ds(x_to, x_count), pl.ds(z_to, z_count)],
                    send_sem=plane_send.at[slab, k], recv_sem=plane_recv.at[slab, k],
                    device_id=at_plane(sx, sz), device_id_type=MESH,
                )
            ))
        return made

    def share(slab):
        for q in range(2):
            for slots, zp, base in ((FINE_SLOTS, 4, 0), (COARSE_SLOTS, 2, 128)):
                for z in range(zp):
                    start = base + (q * zp + z) * 16
                    halo[slab, 1 + q, slots[1 + z]] = own[slab, start : start + 16, :].astype(BF16)
        copies = plane_copies(slab)
        for sx, sz, copy in copies:

            @pl.when(in_plane(sx, sz))
            def _():
                copy.start()

        return copies

    def use(slab, copies):
        for sx, sz, copy in copies:

            @pl.when(in_plane(-sx, -sz))
            def _():
                copy.wait_recv()

        shift_tiles(halo.at[slab], odd, high, low)
        for weights, slots, first, last in (
            (fine_weights, FINE_SLOTS, 0, 128), (coarse_weights, COARSE_SLOTS, 128, 192),
        ):
            given = level(halo.at[slab], odd, high, low, weights, slots, slab)
            if slab == OWN:
                tiles[first:last, :] = given
            else:
                tiles[first:last, :] += given

    def answer(k, when):
        sy, copy = y_copies[k]

        @pl.when(in_y(sy) & jnp.logical_not(waits[sy]) & when)
        def _():
            pl.semaphore_wait(ready.at[k], 1)
            copy.start()

    def receive(k, slab):
        sy, copy = y_copies[k]

        @pl.when(in_y(-sy))
        def _():
            copy.wait_recv()

        spread[k] = got[k].astype(F32)
        for row in range(2):
            at = row if slab == BELOW else 6 + row
            own[slab, pl.ds(at, 24, stride=8), :] = spread[k, pl.ds(row, 24, stride=2), :]

    own_copies = share(OWN)

    @pl.when(gx == 0)
    def _():
        halo[:, 0] = jnp.zeros((3, SLOTS, 16, 128), BF16)

    @pl.when(gx == nx - 1)
    def _():
        halo[:, 3] = jnp.zeros((3, SLOTS, 16, 128), BF16)

    @pl.when(gz == 0)
    def _():
        halo[:, :, 0:2] = jnp.zeros((3, 4, 2, 16, 128), BF16)

    @pl.when(gz == nz - 1)
    def _():
        halo[:, :, 8:10] = jnp.zeros((3, 4, 2, 16, 128), BF16)

    @pl.when(gy == 0)
    def _():
        got[0] = jnp.zeros((48, 128), BF16)

    @pl.when(gy == ny - 1)
    def _():
        got[1] = jnp.zeros((48, 128), BF16)

    loads[2].wait()
    loads[3].wait()
    turn_table(picks, fine_table, turned)
    build_weights(turned, fine_weights)
    loads[4].wait()
    turn_table(picks, coarse_table, turned)
    build_weights(turned, coarse_weights)

    use(OWN, own_copies)
    answer(0, phase < 2)
    answer(1, phase == 3)
    receive(1, ABOVE)
    above_copies = share(ABOVE)
    use(ABOVE, above_copies)
    answer(1, phase == 0)
    receive(0, BELOW)
    below_copies = share(BELOW)
    use(BELOW, below_copies)

    for sy, copy in y_copies:

        @pl.when(in_y(sy))
        def _():
            copy.wait_send()

    for sx, sz, copy in own_copies + above_copies + below_copies:

        @pl.when(in_plane(sx, sz))
        def _():
            copy.wait_send()


def place(tiles, fine_out, coarse_out):
    unpack_level(fine_out, tiles, 8, 0)
    unpack_level(coarse_out, tiles, 4, 128)


def body(sizes, fine_multipoles, fine_translations, coarse_multipoles, coarse_translations):
    vmem = pl.BlockSpec(memory_space=pltpu.VMEM)
    hbm = pl.BlockSpec(memory_space=pl.ANY)
    groups = len(GROUPS)
    tiles = pl.pallas_call(
        functools.partial(kernel, sizes),
        out_shape=pltpu.VMEM((192, 128), F32),
        in_specs=[hbm] * 5,
        out_specs=vmem,
        scratch_shapes=[
            pltpu.VMEM((8 * groups, OFFSETS), BF16),
            pltpu.VMEM(fine_multipoles.shape, BF16),
            pltpu.VMEM(coarse_multipoles.shape, BF16),
            pltpu.VMEM((64, 64, OFFSETS), BF16),
            pltpu.VMEM((64, 64, OFFSETS), BF16),
            pltpu.VMEM((groups * 256, 128), F32),
            pltpu.VMEM((groups, 6, 64, 128), BF16),
            pltpu.VMEM((groups, 6, 64, 128), BF16),
            pltpu.VMEM((3, 4, SLOTS, 16, 128), BF16),
            pltpu.VMEM((3, SLOTS, 16, 128), BF16),
            pltpu.VMEM((2, SLOTS, 16, 128), BF16),
            pltpu.VMEM((2, SLOTS, 16, 128), BF16),
            pltpu.VMEM((128, 128), F32),
            pltpu.VMEM((3, 192, 128), F32),
            pltpu.VMEM((2, 48, 128), F32),
            pltpu.VMEM((2, 48, 128), BF16),
            pltpu.VMEM((2, 48, 128), BF16),
            pltpu.VMEM((2, 48, 128), F32),
            pltpu.SemaphoreType.DMA((5,)),
            pltpu.SemaphoreType.DMA((2,)),
            pltpu.SemaphoreType.DMA((2,)),
            pltpu.SemaphoreType.DMA((3, 8)),
            pltpu.SemaphoreType.DMA((3, 8)),
            pltpu.SemaphoreType.REGULAR((2,)),
        ],
        compiler_params=pltpu.CompilerParams(
            collective_id=0, has_side_effects=True, vmem_limit_bytes=24 * 1024 * 1024
        ),
        name="translate",
    )(*(
        pltpu.with_memory_space_constraint(array, pltpu.HBM)
        for array in (
            jnp.asarray(place_selection(), BF16),
            fine_multipoles,
            jnp.transpose(fine_translations, (1, 2, 0)),
            coarse_multipoles,
            jnp.transpose(coarse_translations, (1, 2, 0)),
        )
    ))
    return pl.pallas_call(
        place,
        out_shape=[
            jax.ShapeDtypeStruct(fine_multipoles.shape, F32),
            jax.ShapeDtypeStruct(coarse_multipoles.shape, F32),
        ],
        in_specs=[vmem],
        out_specs=[vmem, vmem],
        name="place",
    )(pltpu.with_memory_space_constraint(tiles, pltpu.VMEM))


def solution(mesh):
    sizes = tuple(mesh.shape[axis] for axis in ("gx", "gy", "gz"))
    return jax.shard_map(
        functools.partial(body, sizes),
        mesh=mesh,
        in_specs=(P("gx", "gy", "gz", None), P(), P("gx", "gy", "gz", None), P()),
        out_specs=(P("gx", "gy", "gz", None), P("gx", "gy", "gz", None)),
        check_vma=False,
    )
```

```python
import functools

import jax
import jax.numpy as jnp
import numpy as np
from jax import lax
from jax.experimental import pallas as pl
from jax.experimental.pallas import tpu as pltpu
from jax.sharding import PartitionSpec as P

MESH = pl.DeviceIdType.MESH
BF16 = jnp.bfloat16
F32 = jnp.float32

GROUPS = [(0, ey) for ey in range(4)] + [(ex, ey) for ex in range(1, 4) for ey in range(-3, 4)]
OFFSETS = 158
OWN, BELOW, ABOVE = range(3)
Y_PAIRS = (((-3, -2), (-1, 0), (1, 2), (3,)), ((-3, -2), (-1,)), ((1, 2), (3,)))
PLANE = [(-1, -1), (-1, 1), (1, -1), (1, 1), (0, -1), (0, 1), (-1, 0), (1, 0)]
FINE_SLOTS = (0, 2, 4, 5, 6, 8)
COARSE_SLOTS = (1, 3, 7, 9)
SLOTS = 10
TURN = 8


def group(ex, ey):
    return ey if ex == 0 else 4 + (ex - 1) * 7 + ey + 3


def half_offsets():
    listed = []
    for step_x in range(-3, 4):
        for step_y in range(-3, 4):
            for step_z in range(-3, 4):
                if max(abs(step_x), abs(step_y), abs(step_z)) < 2:
                    continue
                if step_x > 0 or (step_x == 0 and (step_y > 0 or (step_y == 0 and step_z > 0))):
                    listed.append((step_x, step_y, step_z))
    return listed


def place_selection():
    picks = np.zeros((8 * len(GROUPS), OFFSETS), np.float32)
    for index, (x, y, z) in enumerate(half_offsets()):
        picks[8 * group(x, y) + z + 3, index] = 1.0
    return picks


def pack_level(src, stage, own, up, down, nz, base, msg_base):
    zp = nz // 2
    stage[0 : 16 * nz, 0:64] = src[...].astype(F32).reshape(16 * nz, 64)
    for x in range(4):
        for y in range(4):
            row = (x * 4 + y) * nz
            even = stage[pl.ds(row, zp, stride=2), 0:64]
            odd = stage[pl.ds(row + 1, zp, stride=2), 0:64]
            both = jnp.concatenate([even, odd], axis=1)
            tile = (x // 2) * zp * 2 + x % 2
            own[pl.ds(base + tile * 8 + 2 + y, zp, stride=16), :] = both
            face = up if y >= 2 else down
            face[pl.ds(msg_base + tile * 2 + y % 2, zp, stride=4), :] = both


def unpack_level(dst, tiles, nz, base):
    zp = nz // 2
    for x in range(4):
        for y in range(4):
            start = base + ((x // 2) * zp * 2 + x % 2) * 8 + y
            both = tiles[pl.ds(start, zp, stride=16), :]
            dst[x, y, pl.ds(0, zp, stride=2), :] = both[:, 0:64]
            dst[x, y, pl.ds(1, zp, stride=2), :] = both[:, 64:128]


def turn_table(picks, table, turned):
    @pl.loop(0, 32 // TURN)
    def _(step):
        for at in range(0, TURN, 2):
            first = step * TURN + at
            rows = jnp.concatenate(
                [table[first], table[32 + first], table[first + 1], table[33 + first]], axis=0
            )
            classes = dot_ahead(picks[...], rows)
            for g in range(len(GROUPS)):
                start = pl.multiple_of(g * 256 + first * 8, 8)
                turned[pl.ds(start, 8), :] = classes[g * 8 : g * 8 + 8, 0:128]
                turned[pl.ds(start + 8, 8), :] = classes[g * 8 : g * 8 + 8, 128:256]


def build_weights(turned, weights):
    left = lax.broadcasted_iota(jnp.int32, (32, 128), 1) < 64

    @pl.loop(0, len(GROUPS) // 5)
    def _(step):
        for at in range(5):
            g = step * 5 + at
            blocks = [turned[pl.ds(g * 256 + e, 32, stride=8), :] for e in range(7)]
            swapped = [pltpu.roll(block, 64, 1) for block in blocks]
            for j in range(6):
                weights[g, j, 0:32] = jnp.where(left, blocks[j], swapped[j + 1]).astype(BF16)
                weights[g, j, 32:64] = jnp.where(left, swapped[j], blocks[j + 1]).astype(BF16)


def ahead(weights, g):
    rows = [jnp.concatenate([weights[g, j + 2 * step] for step in range(3)], axis=1) for j in (1, 0)]
    return jnp.concatenate(rows, axis=0)


def behind(weights, g):
    return jnp.concatenate([weights[g, 5 - s] for s in range(6)], axis=0)


def shift_tiles(halo, odd, high, low):
    zero = jnp.zeros((8, 128), F32)

    @pl.loop(0, SLOTS)
    def _(s):
        wide = [halo[q, s].astype(F32) for q in range(4)]
        for q in range(3):
            odd[q, s] = jnp.concatenate([wide[q][8:16], wide[q + 1][0:8]], axis=0).astype(BF16)
        for q in range(2):
            high[q, s] = jnp.concatenate([wide[q + 2][8:16], zero], axis=0).astype(BF16)
            low[q, s] = jnp.concatenate([zero, wide[q][0:8]], axis=0).astype(BF16)


def sources(halo, odd, high, low, dx, slots):
    if dx % 2 == 0:
        part, first = halo, 1 + dx // 2
    elif dx == 3:
        part, first = high, 0
    elif dx == -3:
        part, first = low, 0
    else:
        part, first = odd, (dx + 1) // 2
    zp = len(slots) - 2
    columns = []
    for step in range(3):
        columns.append(
            jnp.concatenate([part[first + q, slots[z + step]] for q in range(2) for z in range(zp)], axis=0)
        )
    return jnp.concatenate(columns, axis=1)


def dot_ahead(left, weights):
    return lax.dot_general(left, weights, (((1,), (1,)), ((), ())), preferred_element_type=F32)


def dot_behind(left, weights):
    return lax.dot_general(left, weights, (((1,), (0,)), ((), ())), preferred_element_type=F32)


def level(halo, odd, high, low, weights, slots, slab):
    get = functools.partial(sources, halo, odd, high, low, slots=slots)
    forward = {x: get(x) for x in range(0, 4)}
    backward = {x: get(-x) for x in range(0, 4)}
    rows = forward[0].shape[0]
    y = lax.broadcasted_iota(jnp.int32, (rows // 8, 8, 128), 1)
    total = None
    for pair in Y_PAIRS[slab]:
        xs = range(0, 4) if min(pair) >= 0 else range(1, 4)
        left = jnp.concatenate([forward[x] for x in xs], axis=1)
        right = jnp.concatenate(
            [jnp.concatenate([ahead(weights, group(x, ey)) for x in xs], axis=1) for ey in pair], axis=0
        )
        sums = dot_ahead(left, right)
        xs = range(0, 4) if max(pair) <= 0 else range(1, 4)
        left = jnp.concatenate([backward[x] for x in xs], axis=1)
        right = jnp.concatenate(
            [jnp.concatenate([behind(weights, group(x, -ey)) for x in xs], axis=0) for ey in pair], axis=1
        )
        sums = sums + dot_behind(left, right)
        for place, ey in enumerate(pair):
            term = sums[:, place * 128 : place * 128 + 128]
            if ey == 0:
                term = term + dot_ahead(forward[0], ahead(weights, group(0, 0)))
            term = term.reshape(rows // 8, 8, 128)
            term = pltpu.roll(term, (-(2 + ey)) % 8, 1)
            if ey == 3:
                term = jnp.where(y % 2 == 0, term, 0.0)
            if ey == -3:
                term = jnp.where(y % 2 == 1, term, 0.0)
            total = term if total is None else total + term
    return total.reshape(rows, 128)


def kernel(
    sizes, picks_hbm, fine_hbm, fine_table_hbm, coarse_hbm, coarse_table_hbm, tiles,
    picks, fine, coarse, fine_table, coarse_table, turned, fine_weights, coarse_weights,
    halo, odd, high, low, stage, own, faces, sent, got, spread,
    load_sem, y_send, y_recv, plane_send, plane_recv, ready,
):
    nx, ny, nz = sizes
    gx, gy, gz = lax.axis_index("gx"), lax.axis_index("gy"), lax.axis_index("gz")

    loads = [
        pltpu.make_async_copy(src, dst, load_sem.at[k])
        for k, (src, dst) in enumerate((
            (fine_hbm, fine), (coarse_hbm, coarse), (picks_hbm, picks),
            (fine_table_hbm, fine_table), (coarse_table_hbm, coarse_table),
        ))
    ]
    for load in loads:
        load.start()

    def in_y(sy):
        return (gy + sy >= 0) & (gy + sy < ny)

    def in_plane(sx, sz):
        return (gx + sx >= 0) & (gx + sx < nx) & (gz + sz >= 0) & (gz + sz < nz)

    def at_y(sy):
        return (gx, lax.rem(gy + sy + ny, ny), gz)

    def at_plane(sx, sz):
        return (lax.rem(gx + sx + nx, nx), gy, lax.rem(gz + sz + nz, nz))

    phase = lax.rem(gy, 4)
    waits = {1: phase >= 2, -1: (phase == 1) | (phase == 2)}
    barrier = pltpu.get_barrier_semaphore()
    greetings = jnp.int32(0)
    for sy in (1, -1):
        greetings += (in_y(sy) & waits[sy]).astype(jnp.int32)

        @pl.when(in_y(sy) & jnp.logical_not(waits[sy]))
        def _():
            pl.semaphore_signal(barrier, inc=1, device_id=at_y(sy), device_id_type=MESH)

    for sx, sz in PLANE:
        greetings += in_plane(sx, sz).astype(jnp.int32)

        @pl.when(in_plane(sx, sz))
        def _():
            pl.semaphore_signal(barrier, inc=1, device_id=at_plane(sx, sz), device_id_type=MESH)

    loads[0].wait()
    loads[1].wait()
    own[...] = jnp.zeros((3, 192, 128), F32)
    pack_level(fine, stage, own.at[OWN], faces.at[0], faces.at[1], 8, 0, 0)
    pack_level(coarse, stage, own.at[OWN], faces.at[0], faces.at[1], 4, 128, 32)
    sent[...] = faces[...].astype(BF16)

    y_copies = [
        (sy, pltpu.make_async_remote_copy(
            src_ref=sent.at[k], dst_ref=got.at[k], send_sem=y_send.at[k], recv_sem=y_recv.at[k],
            device_id=at_y(sy), device_id_type=MESH,
        ))
        for k, sy in enumerate((1, -1))
    ]
    pl.semaphore_wait(barrier, greetings)
    for k, (sy, copy) in enumerate(y_copies):

        @pl.when(in_y(sy) & waits[sy])
        def _():
            copy.start()
            pl.semaphore_signal(ready.at[1 - k], inc=1, device_id=at_y(sy), device_id_type=MESH)

    def plane_copies(slab):
        made = []
        for k, (sx, sz) in enumerate(PLANE):
            x_from, x_to, x_count = {-1: (1, 3, 1), 0: (1, 1, 2), 1: (2, 0, 1)}[sx]
            z_from, z_to, z_count = {-1: (2, 8, 2), 0: (2, 2, 6), 1: (6, 0, 2)}[sz]
            made.append((
                sx, sz, pltpu.make_async_remote_copy(
                    src_ref=halo.at[slab, pl.ds(x_from, x_count), pl.ds(z_from, z_count)],
                    dst_ref=halo.at[slab, pl.ds(x_to, x_count), pl.ds(z_to, z_count)],
                    send_sem=plane_send.at[slab, k], recv_sem=plane_recv.at[slab, k],
                    device_id=at_plane(sx, sz), device_id_type=MESH,
                )
            ))
        return made

    def share(slab):
        for q in range(2):
            for slots, zp, base in ((FINE_SLOTS, 4, 0), (COARSE_SLOTS, 2, 128)):
                for z in range(zp):
                    start = base + (q * zp + z) * 16
                    halo[slab, 1 + q, slots[1 + z]] = own[slab, start : start + 16, :].astype(BF16)
        copies = plane_copies(slab)
        for sx, sz, copy in copies:

            @pl.when(in_plane(sx, sz))
            def _():
                copy.start()

        return copies

    def use(slab, copies):
        for sx, sz, copy in copies:

            @pl.when(in_plane(-sx, -sz))
            def _():
                copy.wait_recv()

        shift_tiles(halo.at[slab], odd, high, low)
        for weights, slots, first, last in (
            (fine_weights, FINE_SLOTS, 0, 128), (coarse_weights, COARSE_SLOTS, 128, 192),
        ):
            given = level(halo.at[slab], odd, high, low, weights, slots, slab)
            if slab == OWN:
                tiles[first:last, :] = given
            else:
                tiles[first:last, :] += given
        for sx, sz, copy in copies:

            @pl.when(in_plane(sx, sz))
            def _():
                copy.wait_send()

    def answer(k, when):
        sy, copy = y_copies[k]

        @pl.when(in_y(sy) & jnp.logical_not(waits[sy]) & when)
        def _():
            pl.semaphore_wait(ready.at[k], 1)
            copy.start()

    def receive(k, slab):
        sy, copy = y_copies[k]

        @pl.when(in_y(-sy))
        def _():
            copy.wait_recv()

        spread[k] = got[k].astype(F32)
        for row in range(2):
            at = row if slab == BELOW else 6 + row
            own[slab, pl.ds(at, 24, stride=8), :] = spread[k, pl.ds(row, 24, stride=2), :]

    own_copies = share(OWN)

    @pl.when(gx == 0)
    def _():
        halo[:, 0] = jnp.zeros((3, SLOTS, 16, 128), BF16)

    @pl.when(gx == nx - 1)
    def _():
        halo[:, 3] = jnp.zeros((3, SLOTS, 16, 128), BF16)

    @pl.when(gz == 0)
    def _():
        halo[:, :, 0:2] = jnp.zeros((3, 4, 2, 16, 128), BF16)

    @pl.when(gz == nz - 1)
    def _():
        halo[:, :, 8:10] = jnp.zeros((3, 4, 2, 16, 128), BF16)

    loads[2].wait()
    loads[3].wait()
    turn_table(picks, fine_table, turned)
    build_weights(turned, fine_weights)
    loads[4].wait()
    turn_table(picks, coarse_table, turned)
    build_weights(turned, coarse_weights)

    use(OWN, own_copies)
    answer(0, phase < 2)
    answer(1, phase == 3)

    @pl.loop(0, 2)
    def _(step):
        above = (step == 0) == (phase == 0)

        @pl.when(above & in_y(1))
        def _():
            receive(1, ABOVE)
            use(ABOVE, share(ABOVE))

        @pl.when(jnp.logical_not(above) & in_y(-1))
        def _():
            answer(1, phase == 0)
            receive(0, BELOW)
            use(BELOW, share(BELOW))

    for sy, copy in y_copies:

        @pl.when(in_y(sy))
        def _():
            copy.wait_send()


def place(tiles, fine_out, coarse_out):
    unpack_level(fine_out, tiles, 8, 0)
    unpack_level(coarse_out, tiles, 4, 128)


def body(sizes, fine_multipoles, fine_translations, coarse_multipoles, coarse_translations):
    vmem = pl.BlockSpec(memory_space=pltpu.VMEM)
    hbm = pl.BlockSpec(memory_space=pl.ANY)
    groups = len(GROUPS)
    tiles = pl.pallas_call(
        functools.partial(kernel, sizes),
        out_shape=pltpu.VMEM((192, 128), F32),
        in_specs=[hbm] * 5,
        out_specs=vmem,
        scratch_shapes=[
            pltpu.VMEM((8 * groups, OFFSETS), BF16),
            pltpu.VMEM(fine_multipoles.shape, BF16),
            pltpu.VMEM(coarse_multipoles.shape, BF16),
            pltpu.VMEM((64, 64, OFFSETS), BF16),
            pltpu.VMEM((64, 64, OFFSETS), BF16),
            pltpu.VMEM((groups * 256, 128), F32),
            pltpu.VMEM((groups, 6, 64, 128), BF16),
            pltpu.VMEM((groups, 6, 64, 128), BF16),
            pltpu.VMEM((3, 4, SLOTS, 16, 128), BF16),
            pltpu.VMEM((3, SLOTS, 16, 128), BF16),
            pltpu.VMEM((2, SLOTS, 16, 128), BF16),
            pltpu.VMEM((2, SLOTS, 16, 128), BF16),
            pltpu.VMEM((128, 128), F32),
            pltpu.VMEM((3, 192, 128), F32),
            pltpu.VMEM((2, 48, 128), F32),
            pltpu.VMEM((2, 48, 128), BF16),
            pltpu.VMEM((2, 48, 128), BF16),
            pltpu.VMEM((2, 48, 128), F32),
            pltpu.SemaphoreType.DMA((5,)),
            pltpu.SemaphoreType.DMA((2,)),
            pltpu.SemaphoreType.DMA((2,)),
            pltpu.SemaphoreType.DMA((3, 8)),
            pltpu.SemaphoreType.DMA((3, 8)),
            pltpu.SemaphoreType.REGULAR((2,)),
        ],
        compiler_params=pltpu.CompilerParams(
            collective_id=0, has_side_effects=True, vmem_limit_bytes=24 * 1024 * 1024
        ),
        name="translate",
    )(*(
        pltpu.with_memory_space_constraint(array, pltpu.HBM)
        for array in (
            jnp.asarray(place_selection(), BF16),
            fine_multipoles,
            jnp.transpose(fine_translations, (1, 2, 0)),
            coarse_multipoles,
            jnp.transpose(coarse_translations, (1, 2, 0)),
        )
    ))
    return pl.pallas_call(
        place,
        out_shape=[
            jax.ShapeDtypeStruct(fine_multipoles.shape, F32),
            jax.ShapeDtypeStruct(coarse_multipoles.shape, F32),
        ],
        in_specs=[vmem],
        out_specs=[vmem, vmem],
        name="place",
    )(pltpu.with_memory_space_constraint(tiles, pltpu.VMEM))


def solution(mesh):
    sizes = tuple(mesh.shape[axis] for axis in ("gx", "gy", "gz"))
    return jax.shard_map(
        functools.partial(body, sizes),
        mesh=mesh,
        in_specs=(P("gx", "gy", "gz", None), P(), P("gx", "gy", "gz", None), P()),
        out_specs=(P("gx", "gy", "gz", None), P("gx", "gy", "gz", None)),
        check_vma=False,
    )
```

```python
import functools

import jax
import jax.numpy as jnp
import numpy as np
from jax import lax
from jax.experimental import pallas as pl
from jax.experimental.pallas import tpu as pltpu
from jax.sharding import PartitionSpec as P

MESH = pl.DeviceIdType.MESH
BF16 = jnp.bfloat16
F32 = jnp.float32

GROUPS = [(0, ey) for ey in range(4)] + [(ex, ey) for ex in range(1, 4) for ey in range(-3, 4)]
OFFSETS = 158
OWN, BELOW, ABOVE = range(3)
Y_PAIRS = (((-3, -2), (-1, 0), (1, 2), (3,)), ((-3, -2), (-1,)), ((1, 2), (3,)))
PLANE = [(-1, -1), (-1, 1), (1, -1), (1, 1), (0, -1), (0, 1), (-1, 0), (1, 0)]
FINE_SLOTS = (0, 2, 4, 5, 6, 8)
COARSE_SLOTS = (1, 3, 7, 9)
SLOTS = 10
TURN = 8


def group(ex, ey):
    return ey if ex == 0 else 4 + (ex - 1) * 7 + ey + 3


def half_offsets():
    listed = []
    for step_x in range(-3, 4):
        for step_y in range(-3, 4):
            for step_z in range(-3, 4):
                if max(abs(step_x), abs(step_y), abs(step_z)) < 2:
                    continue
                if step_x > 0 or (step_x == 0 and (step_y > 0 or (step_y == 0 and step_z > 0))):
                    listed.append((step_x, step_y, step_z))
    return listed


def place_selection():
    picks = np.zeros((8 * len(GROUPS), OFFSETS), np.float32)
    for index, (x, y, z) in enumerate(half_offsets()):
        picks[8 * group(x, y) + z + 3, index] = 1.0
    return picks


def pack_level(src, stage, own, up, down, nz, base, msg_base):
    zp = nz // 2
    stage[0 : 16 * nz, 0:64] = src[...].astype(F32).reshape(16 * nz, 64)
    for x in range(4):
        for y in range(4):
            row = (x * 4 + y) * nz
            even = stage[pl.ds(row, zp, stride=2), 0:64]
            odd = stage[pl.ds(row + 1, zp, stride=2), 0:64]
            both = jnp.concatenate([even, odd], axis=1)
            tile = (x // 2) * zp * 2 + x % 2
            own[pl.ds(base + tile * 8 + 2 + y, zp, stride=16), :] = both
            face = up if y >= 2 else down
            face[pl.ds(msg_base + tile * 2 + y % 2, zp, stride=4), :] = both


def unpack_level(dst, tiles, nz, base):
    zp = nz // 2
    for x in range(4):
        for y in range(4):
            start = base + ((x // 2) * zp * 2 + x % 2) * 8 + y
            both = tiles[pl.ds(start, zp, stride=16), :]
            dst[x, y, pl.ds(0, zp, stride=2), :] = both[:, 0:64]
            dst[x, y, pl.ds(1, zp, stride=2), :] = both[:, 64:128]


def turn_table(picks, table, turned):
    @pl.loop(0, 32 // TURN)
    def _(step):
        for at in range(0, TURN, 2):
            first = step * TURN + at
            rows = jnp.concatenate(
                [table[first], table[32 + first], table[first + 1], table[33 + first]], axis=0
            )
            classes = dot_ahead(picks[...], rows)
            for g in range(len(GROUPS)):
                start = pl.multiple_of(g * 256 + first * 8, 8)
                turned[pl.ds(start, 8), :] = classes[g * 8 : g * 8 + 8, 0:128]
                turned[pl.ds(start + 8, 8), :] = classes[g * 8 : g * 8 + 8, 128:256]


def build_weights(turned, weights):
    left = lax.broadcasted_iota(jnp.int32, (32, 128), 1) < 64

    @pl.loop(0, len(GROUPS) // 5)
    def _(step):
        for at in range(5):
            g = step * 5 + at
            blocks = [turned[pl.ds(g * 256 + e, 32, stride=8), :] for e in range(7)]
            swapped = [pltpu.roll(block, 64, 1) for block in blocks]
            for j in range(6):
                weights[g, j, 0:32] = jnp.where(left, blocks[j], swapped[j + 1]).astype(BF16)
                weights[g, j, 32:64] = jnp.where(left, swapped[j], blocks[j + 1]).astype(BF16)


def ahead(weights, g):
    rows = [jnp.concatenate([weights[g, j + 2 * step] for step in range(3)], axis=1) for j in (1, 0)]
    return jnp.concatenate(rows, axis=0)


def behind(weights, g):
    return jnp.concatenate([weights[g, 5 - s] for s in range(6)], axis=0)


def shift_tiles(halo, odd, high, low):
    zero = jnp.zeros((8, 128), F32)

    @pl.loop(0, SLOTS)
    def _(s):
        wide = [halo[q, s].astype(F32) for q in range(4)]
        for q in range(3):
            odd[q, s] = jnp.concatenate([wide[q][8:16], wide[q + 1][0:8]], axis=0).astype(BF16)
        for q in range(2):
            high[q, s] = jnp.concatenate([wide[q + 2][8:16], zero], axis=0).astype(BF16)
            low[q, s] = jnp.concatenate([zero, wide[q][0:8]], axis=0).astype(BF16)


def sources(halo, odd, high, low, dx, slots):
    if dx % 2 == 0:
        part, first = halo, 1 + dx // 2
    elif dx == 3:
        part, first = high, 0
    elif dx == -3:
        part, first = low, 0
    else:
        part, first = odd, (dx + 1) // 2
    zp = len(slots) - 2
    columns = []
    for step in range(3):
        columns.append(
            jnp.concatenate([part[first + q, slots[z + step]] for q in range(2) for z in range(zp)], axis=0)
        )
    return jnp.concatenate(columns, axis=1)


def dot_ahead(left, weights):
    return lax.dot_general(left, weights, (((1,), (1,)), ((), ())), preferred_element_type=F32)


def dot_behind(left, weights):
    return lax.dot_general(left, weights, (((1,), (0,)), ((), ())), preferred_element_type=F32)


def level(halo, odd, high, low, weights, slots, slab):
    get = functools.partial(sources, halo, odd, high, low, slots=slots)
    forward = {x: get(x) for x in range(0, 4)}
    backward = {x: get(-x) for x in range(0, 4)}
    rows = forward[0].shape[0]
    y = lax.broadcasted_iota(jnp.int32, (rows // 8, 8, 128), 1)
    total = None
    for pair in Y_PAIRS[slab]:
        xs = range(0, 4) if min(pair) >= 0 else range(1, 4)
        left = jnp.concatenate([forward[x] for x in xs], axis=1)
        right = jnp.concatenate(
            [jnp.concatenate([ahead(weights, group(x, ey)) for x in xs], axis=1) for ey in pair], axis=0
        )
        sums = dot_ahead(left, right)
        xs = range(0, 4) if max(pair) <= 0 else range(1, 4)
        left = jnp.concatenate([backward[x] for x in xs], axis=1)
        right = jnp.concatenate(
            [jnp.concatenate([behind(weights, group(x, -ey)) for x in xs], axis=0) for ey in pair], axis=1
        )
        sums = sums + dot_behind(left, right)
        for place, ey in enumerate(pair):
            term = sums[:, place * 128 : place * 128 + 128]
            if ey == 0:
                term = term + dot_ahead(forward[0], ahead(weights, group(0, 0)))
            term = term.reshape(rows // 8, 8, 128)
            term = pltpu.roll(term, (-(2 + ey)) % 8, 1)
            if ey == 3:
                term = jnp.where(y % 2 == 0, term, 0.0)
            if ey == -3:
                term = jnp.where(y % 2 == 1, term, 0.0)
            total = term if total is None else total + term
    return total.reshape(rows, 128)


def kernel(
    sizes, picks_hbm, fine_hbm, fine_table_hbm, coarse_hbm, coarse_table_hbm, tiles,
    picks, fine, coarse, fine_table, coarse_table, turned, fine_weights, coarse_weights,
    halo, odd, high, low, stage, own, faces, sent, got, spread,
    load_sem, y_send, y_recv, plane_send, plane_recv, ready,
):
    nx, ny, nz = sizes
    gx, gy, gz = lax.axis_index("gx"), lax.axis_index("gy"), lax.axis_index("gz")

    loads = [
        pltpu.make_async_copy(src, dst, load_sem.at[k])
        for k, (src, dst) in enumerate((
            (fine_hbm, fine), (coarse_hbm, coarse), (picks_hbm, picks),
            (fine_table_hbm, fine_table), (coarse_table_hbm, coarse_table),
        ))
    ]
    for load in loads:
        load.start()

    def in_y(sy):
        return (gy + sy >= 0) & (gy + sy < ny)

    def in_plane(sx, sz):
        return (gx + sx >= 0) & (gx + sx < nx) & (gz + sz >= 0) & (gz + sz < nz)

    def at_y(sy):
        return (gx, lax.rem(gy + sy + ny, ny), gz)

    def at_plane(sx, sz):
        return (lax.rem(gx + sx + nx, nx), gy, lax.rem(gz + sz + nz, nz))

    phase = lax.rem(gy, 4)
    waits = {1: phase >= 2, -1: (phase == 1) | (phase == 2)}
    barrier = pltpu.get_barrier_semaphore()
    greetings = jnp.int32(0)
    for sy in (1, -1):
        greetings += (in_y(sy) & waits[sy]).astype(jnp.int32)

        @pl.when(in_y(sy) & jnp.logical_not(waits[sy]))
        def _():
            pl.semaphore_signal(barrier, inc=1, device_id=at_y(sy), device_id_type=MESH)

    for sx, sz in PLANE:
        greetings += in_plane(sx, sz).astype(jnp.int32)

        @pl.when(in_plane(sx, sz))
        def _():
            pl.semaphore_signal(barrier, inc=1, device_id=at_plane(sx, sz), device_id_type=MESH)

    loads[0].wait()
    loads[1].wait()
    own[...] = jnp.zeros((3, 192, 128), F32)
    pack_level(fine, stage, own.at[OWN], faces.at[0], faces.at[1], 8, 0, 0)
    pack_level(coarse, stage, own.at[OWN], faces.at[0], faces.at[1], 4, 128, 32)
    sent[...] = faces[...].astype(BF16)

    y_copies = [
        (sy, pltpu.make_async_remote_copy(
            src_ref=sent.at[k], dst_ref=got.at[k], send_sem=y_send.at[k], recv_sem=y_recv.at[k],
            device_id=at_y(sy), device_id_type=MESH,
        ))
        for k, sy in enumerate((1, -1))
    ]
    pl.semaphore_wait(barrier, greetings)
    for k, (sy, copy) in enumerate(y_copies):

        @pl.when(in_y(sy) & waits[sy])
        def _():
            copy.start()
            pl.semaphore_signal(ready.at[1 - k], inc=1, device_id=at_y(sy), device_id_type=MESH)

    def plane_copies(slab):
        made = []
        for k, (sx, sz) in enumerate(PLANE):
            x_from, x_to, x_count = {-1: (1, 3, 1), 0: (1, 1, 2), 1: (2, 0, 1)}[sx]
            z_from, z_to, z_count = {-1: (2, 8, 2), 0: (2, 2, 6), 1: (6, 0, 2)}[sz]
            made.append((
                sx, sz, pltpu.make_async_remote_copy(
                    src_ref=halo.at[slab, pl.ds(x_from, x_count), pl.ds(z_from, z_count)],
                    dst_ref=halo.at[slab, pl.ds(x_to, x_count), pl.ds(z_to, z_count)],
                    send_sem=plane_send.at[slab, k], recv_sem=plane_recv.at[slab, k],
                    device_id=at_plane(sx, sz), device_id_type=MESH,
                )
            ))
        return made

    def share(slab):
        for q in range(2):
            for slots, zp, base in ((FINE_SLOTS, 4, 0), (COARSE_SLOTS, 2, 128)):
                for z in range(zp):
                    start = base + (q * zp + z) * 16
                    halo[slab, 1 + q, slots[1 + z]] = own[slab, start : start + 16, :].astype(BF16)
        copies = plane_copies(slab)
        for sx, sz, copy in copies:

            @pl.when(in_plane(sx, sz))
            def _():
                copy.start()

        return copies

    def use(slab, copies):
        for sx, sz, copy in copies:

            @pl.when(in_plane(-sx, -sz))
            def _():
                copy.wait_recv()

        shift_tiles(halo.at[slab], odd, high, low)
        for weights, slots, first, last in (
            (fine_weights, FINE_SLOTS, 0, 128), (coarse_weights, COARSE_SLOTS, 128, 192),
        ):
            given = level(halo.at[slab], odd, high, low, weights, slots, slab)
            if slab == OWN:
                tiles[first:last, :] = given
            else:
                tiles[first:last, :] += given
        for sx, sz, copy in copies:

            @pl.when(in_plane(sx, sz))
            def _():
                copy.wait_send()

    def answer(k, when):
        sy, copy = y_copies[k]

        @pl.when(in_y(sy) & jnp.logical_not(waits[sy]) & when)
        def _():
            pl.semaphore_wait(ready.at[k], 1)
            copy.start()

    def receive(k, slab):
        sy, copy = y_copies[k]

        @pl.when(in_y(-sy))
        def _():
            copy.wait_recv()

        spread[k] = got[k].astype(F32)
        for row in range(2):
            at = row if slab == BELOW else 6 + row
            own[slab, pl.ds(at, 24, stride=8), :] = spread[k, pl.ds(row, 24, stride=2), :]

    own_copies = share(OWN)

    @pl.when(gx == 0)
    def _():
        halo[:, 0] = jnp.zeros((3, SLOTS, 16, 128), BF16)

    @pl.when(gx == nx - 1)
    def _():
        halo[:, 3] = jnp.zeros((3, SLOTS, 16, 128), BF16)

    @pl.when(gz == 0)
    def _():
        halo[:, :, 0:2] = jnp.zeros((3, 4, 2, 16, 128), BF16)

    @pl.when(gz == nz - 1)
    def _():
        halo[:, :, 8:10] = jnp.zeros((3, 4, 2, 16, 128), BF16)

    loads[2].wait()
    loads[3].wait()
    turn_table(picks, fine_table, turned)
    build_weights(turned, fine_weights)
    loads[4].wait()
    turn_table(picks, coarse_table, turned)
    build_weights(turned, coarse_weights)

    use(OWN, own_copies)
    answer(0, phase == 0)
    answer(1, phase == 3)

    @pl.loop(0, 2)
    def _(step):
        above = (step == 0) == (phase == 0)

        @pl.when(above & in_y(1))
        def _():
            answer(0, phase == 1)
            receive(1, ABOVE)
            use(ABOVE, share(ABOVE))

        @pl.when(jnp.logical_not(above) & in_y(-1))
        def _():
            answer(1, phase == 0)
            receive(0, BELOW)
            use(BELOW, share(BELOW))

    for sy, copy in y_copies:

        @pl.when(in_y(sy))
        def _():
            copy.wait_send()


def place(tiles, fine_out, coarse_out):
    unpack_level(fine_out, tiles, 8, 0)
    unpack_level(coarse_out, tiles, 4, 128)


def body(sizes, fine_multipoles, fine_translations, coarse_multipoles, coarse_translations):
    vmem = pl.BlockSpec(memory_space=pltpu.VMEM)
    hbm = pl.BlockSpec(memory_space=pl.ANY)
    groups = len(GROUPS)
    tiles = pl.pallas_call(
        functools.partial(kernel, sizes),
        out_shape=pltpu.VMEM((192, 128), F32),
        in_specs=[hbm] * 5,
        out_specs=vmem,
        scratch_shapes=[
            pltpu.VMEM((8 * groups, OFFSETS), BF16),
            pltpu.VMEM(fine_multipoles.shape, BF16),
            pltpu.VMEM(coarse_multipoles.shape, BF16),
            pltpu.VMEM((64, 64, OFFSETS), BF16),
            pltpu.VMEM((64, 64, OFFSETS), BF16),
            pltpu.VMEM((groups * 256, 128), F32),
            pltpu.VMEM((groups, 6, 64, 128), BF16),
            pltpu.VMEM((groups, 6, 64, 128), BF16),
            pltpu.VMEM((3, 4, SLOTS, 16, 128), BF16),
            pltpu.VMEM((3, SLOTS, 16, 128), BF16),
            pltpu.VMEM((2, SLOTS, 16, 128), BF16),
            pltpu.VMEM((2, SLOTS, 16, 128), BF16),
            pltpu.VMEM((128, 128), F32),
            pltpu.VMEM((3, 192, 128), F32),
            pltpu.VMEM((2, 48, 128), F32),
            pltpu.VMEM((2, 48, 128), BF16),
            pltpu.VMEM((2, 48, 128), BF16),
            pltpu.VMEM((2, 48, 128), F32),
            pltpu.SemaphoreType.DMA((5,)),
            pltpu.SemaphoreType.DMA((2,)),
            pltpu.SemaphoreType.DMA((2,)),
            pltpu.SemaphoreType.DMA((3, 8)),
            pltpu.SemaphoreType.DMA((3, 8)),
            pltpu.SemaphoreType.REGULAR((2,)),
        ],
        compiler_params=pltpu.CompilerParams(
            collective_id=0, has_side_effects=True, vmem_limit_bytes=24 * 1024 * 1024
        ),
        name="translate",
    )(*(
        pltpu.with_memory_space_constraint(array, pltpu.HBM)
        for array in (
            jnp.asarray(place_selection(), BF16),
            fine_multipoles,
            jnp.transpose(fine_translations, (1, 2, 0)),
            coarse_multipoles,
            jnp.transpose(coarse_translations, (1, 2, 0)),
        )
    ))
    return pl.pallas_call(
        place,
        out_shape=[
            jax.ShapeDtypeStruct(fine_multipoles.shape, F32),
            jax.ShapeDtypeStruct(coarse_multipoles.shape, F32),
        ],
        in_specs=[vmem],
        out_specs=[vmem, vmem],
        name="place",
    )(pltpu.with_memory_space_constraint(tiles, pltpu.VMEM))


def solution(mesh):
    sizes = tuple(mesh.shape[axis] for axis in ("gx", "gy", "gz"))
    return jax.shard_map(
        functools.partial(body, sizes),
        mesh=mesh,
        in_specs=(P("gx", "gy", "gz", None), P(), P("gx", "gy", "gz", None), P()),
        out_specs=(P("gx", "gy", "gz", None), P("gx", "gy", "gz", None)),
        check_vma=False,
    )
```
